32 devices in a mesh: docs: 8 (over z, x), seq: 4 (over y, core).
Axes of the slice: x: 2, y: 2, z: 4, core: 2. Of those that a mesh axis runs over, the one named last changes fastest.
Arguments:
- tokens: bfloat16 [8, 1024, 1024], P('docs', 'seq'), may hold values from -6 to 6
- cotangent: bfloat16 [8, 1024, 1024], P('docs', 'seq'), may hold values from -6 to 6
- cache_keys: bfloat16 [8, 2048, 1024], P(None, ('docs', 'seq')), may hold values from -6 to 6
- cache_values: bfloat16 [8, 2048, 1024], P(None, ('docs', 'seq')), may hold values from -6 to 6
- neighbours: int32 [8, 1024, 64], P('docs', 'seq'), may hold values from 0 to 4095
- partner: int32 [8], replicated, may hold values from 0 to 7, as said below
- has_memory: int32 [8], replicated, may hold values from 0 to 1, as said below
- w_heads: float32 [1024, 3072], P(('docs', 'seq')), may hold values from -0.1875 to 0.1875
- moment_heads: float32 [1024, 3072], P(('docs', 'seq')), may hold values from -0.0004272461 to 0.0004272461
- square_heads: float32 [1024, 3072], P(('docs', 'seq')), may hold values from 8e-11 to 3.2e-10
- w_merge: float32 [1024, 1024], P(('docs', 'seq')), may hold values from -1.5 to 1.5
- moment_merge: float32 [1024, 1024], P(('docs', 'seq')), may hold values from -0.0004272461 to 0.0004272461
- square_merge: float32 [1024, 1024], P(('docs', 'seq')), may hold values from 4.671058e-12 to 1.8684231e-11
- w_gate: float32 [1024, 2816], P(('docs', 'seq')), may hold values from -0.1875 to 0.1875
- moment_gate: float32 [1024, 2816], P(('docs', 'seq')), may hold values from -0.0004272461 to 0.0004272461
- square_gate: float32 [1024, 2816], P(('docs', 'seq')), may hold values from 8e-11 to 3.2e-10
- w_up: float32 [1024, 2816], P(('docs', 'seq')), may hold values from -0.1875 to 0.1875
- moment_up: float32 [1024, 2816], P(('docs', 'seq')), may hold values from -0.0004272461 to 0.0004272461
- square_up: float32 [1024, 2816], P(('docs', 'seq')), may hold values from 8e-11 to 3.2e-10
- w_down: float32 [2816, 1024], P(('docs', 'seq')), may hold values from -0.109375 to 0.109375
- moment_down: float32 [2816, 1024], P(('docs', 'seq')), may hold values from -0.0004272461 to 0.0004272461
- square_down: float32 [2816, 1024], P(('docs', 'seq')), may hold values from 8e-11 to 3.2e-10
- gains: float32 [2, 1024], P(None, ('docs', 'seq')), may hold values from 0.25 to 3
- moment_gains: float32 [2, 1024], P(None, ('docs', 'seq')), may hold values from -0.0008544922 to 0.0008544922
- square_gains: float32 [2, 1024], P(None, ('docs', 'seq')), may hold values from 2e-10 to 8e-10
Outputs:
- activations: bfloat16 [8, 1024, 1024], P('docs', 'seq')
- input_grad: float32 [8, 1024, 1024], P('docs', 'seq')
- heads_moment: float32 [1024, 3072], P(('docs', 'seq'))
- heads_square: float32 [1024, 3072], P(('docs', 'seq'))
- heads_weight: float32 [1024, 3072], P(('docs', 'seq'))
- merge_moment: float32 [1024, 1024], P(('docs', 'seq'))
- merge_square: float32 [1024, 1024], P(('docs', 'seq'))
- merge_weight: float32 [1024, 1024], P(('docs', 'seq'))
- gate_moment: float32 [1024, 2816], P(('docs', 'seq'))
- gate_square: float32 [1024, 2816], P(('docs', 'seq'))
- gate_weight: float32 [1024, 2816], P(('docs', 'seq'))
- up_moment: float32 [1024, 2816], P(('docs', 'seq'))
- up_square: float32 [1024, 2816], P(('docs', 'seq'))
- up_weight: float32 [1024, 2816], P(('docs', 'seq'))
- down_moment: float32 [2816, 1024], P(('docs', 'seq'))
- down_square: float32 [2816, 1024], P(('docs', 'seq'))
- down_weight: float32 [2816, 1024], P(('docs', 'seq'))
- gains_moment: float32 [2, 1024], P(None, ('docs', 'seq'))
- gains_square: float32 [2, 1024], P(None, ('docs', 'seq'))
- gains_weight: float32 [2, 1024], P(None, ('docs', 'seq'))
- clip_norm: float32 [], replicated
- layer_norms: float32 [2, 6], replicated
The draws below stay inside these ranges and needn't reach their ends.
Inputs may be any that keep to these rules, and one draw needn't show every extreme that they name: Exactly half of the documents have memory; a document with memory has as partner another document with memory and partners are mutual; a document without memory is its own partner. `has_memory`: exactly half of the 8 documents have memory. `neighbours`: indices below 2048 name keys of the document's own cache, the others keys of its partner's cache; they are read only for documents with memory.
All inputs are finite; a program needn't handle non-finite values.
Results may differ from the reference program's by a relative error of at most 0.015.
Values may be sent and summed in bfloat16 or wider, within the bound.
No kernel may reach another device: no remote copies, remote signals or barrier semaphores. Data moves between devices by JAX's collectives and lax.ppermute only.
A program may use at most 256 MiB of HBM per device.

```python
import math
import jax
import jax.numpy as jnp
from jax import lax

D = 1024
HEADS = 8
HEAD_DIM = 128
FF = 2816
MEM = 2048
KNN = 64
STEP = 10
DOCS = 8
LEN = 1024


def memory_order(key):
    order = jax.random.permutation(key, DOCS).astype(jnp.int32)
    ranking = jnp.argsort(order).astype(jnp.int32)
    return (order, ranking)


def draw_has_memory(key, part):
    order, ranking = memory_order(key)
    return (ranking < DOCS // 2).astype(jnp.int32)


def draw_partner(key, part):
    order, ranking = memory_order(key)
    mate_doc = order[jnp.bitwise_xor(ranking, 1)]
    return jnp.where(ranking < DOCS // 2, mate_doc, jnp.arange(DOCS, dtype=jnp.int32)).astype(jnp.int32)


def draw_gains(key, part):
    key = jax.random.fold_in(key, 11)
    place = jnp.arange(D, dtype=jnp.float32) / D
    ramp = 0.6 * 3.0 ** place
    rough = 1.0 + 0.05 * jax.random.normal(key, (2, D), jnp.float32)
    return (ramp[None, :] * rough).astype(jnp.float32)


def place_ends(values, key, low, largest):
    longest = values.shape.index(max(values.shape))
    spots = []
    for shift in (0, 1):
        where = [jax.random.randint(jax.random.fold_in(key, axis), (), 0, length) for axis, length in enumerate(values.shape)]
        where[longest] = (where[longest] + shift) % values.shape[longest]
        spots.append(tuple(where))
    return values.at[spots[0]].set(low).at[spots[1]].set(largest)


def shard_levels(rng, shape, cuts, least, high):
    gain = 1.0
    for axis_at, blocks in cuts:
        steps = jax.random.uniform(jax.random.fold_in(jax.random.fold_in(rng, 6), axis_at), (blocks,), jnp.float32, least / len(cuts), high / len(cuts))
        gain = gain * jnp.repeat(jnp.exp(steps), shape[axis_at] // blocks).reshape((-1,) + (1,) * (len(shape) - 1 - axis_at))
    return gain


def noise(stream_key, extent, scale, most, shards=(), kind=jnp.bfloat16):
    entries = scale * jax.random.normal(stream_key, extent, jnp.float32)
    if shards:
        entries = entries * shard_levels(stream_key, extent, shards, -0.22, 0.18)
    return jnp.clip(entries, -most, most).astype(kind)


def setup_inputs(seed: int = 0) -> dict:
    streams_of = jax.random.split(jax.random.key(seed), 26)
    tokens = noise(streams_of[0], (DOCS, LEN, D), 1.0, 6.0, ((0, 8), (1, 4)))
    cotangent = noise(streams_of[1], (DOCS, LEN, D), 1.0, 6.0, ((0, 8), (1, 4)))
    cache_keys = noise(streams_of[2], (DOCS, MEM, D), 1.0, 6.0, ((1, 32),))
    cache_values = noise(streams_of[3], (DOCS, MEM, D), 1.0, 6.0, ((1, 32),))
    neighbours = place_ends(jax.random.randint(streams_of[4], (DOCS, LEN, KNN), 0, 2 * MEM), jax.random.fold_in(streams_of[4], 1), 0, (2 * MEM) - 1).astype(jnp.int32)
    partner = draw_partner(jax.random.fold_in(streams_of[25], 71), 0)
    has_memory = draw_has_memory(jax.random.fold_in(streams_of[25], 71), 0)
    w_heads = noise(streams_of[7], (D, 3 * D), D ** -0.5, 0.1875, ((0, 32),), jnp.float32)
    moment_heads = noise(streams_of[8], (D, 3 * D), 0.00003, 0.0004272461, ((0, 32),), jnp.float32)
    square_heads = jnp.clip(jnp.exp(math.log(3.199999987213431e-10) - 1.3862944 * jax.random.uniform(streams_of[9], (D, 3 * D), jnp.float32) ** shard_levels(streams_of[9], (D, 3 * D), ((0, 32),), -0.2, 0.2)), 7.999999968033578e-11, 3.199999987213431e-10)
    w_merge = noise(streams_of[10], (D, D), (D // 64) ** -0.5, 1.5, ((0, 32),), jnp.float32)
    moment_merge = noise(streams_of[11], (D, D), 0.00003, 0.0004272461, ((0, 32),), jnp.float32)
    square_merge = jnp.clip(jnp.exp(math.log(1.868423124551377e-11) - 1.3862944 * jax.random.uniform(streams_of[12], (D, D), jnp.float32) ** shard_levels(streams_of[12], (D, D), ((0, 32),), -0.2, 0.2)), 4.671057811378443e-12, 1.868423124551377e-11)
    w_gate = noise(streams_of[13], (D, FF), D ** -0.5, 0.1875, ((0, 32),), jnp.float32)
    moment_gate = noise(streams_of[14], (D, FF), 0.00003, 0.0004272461, ((0, 32),), jnp.float32)
    square_gate = jnp.clip(jnp.exp(math.log(3.199999987213431e-10) - 1.3862944 * jax.random.uniform(streams_of[15], (D, FF), jnp.float32) ** shard_levels(streams_of[15], (D, FF), ((0, 32),), -0.2, 0.2)), 7.999999968033578e-11, 3.199999987213431e-10)
    w_up = noise(streams_of[16], (D, FF), D ** -0.5, 0.1875, ((0, 32),), jnp.float32)
    moment_up = noise(streams_of[17], (D, FF), 0.00003, 0.0004272461, ((0, 32),), jnp.float32)
    square_up = jnp.clip(jnp.exp(math.log(3.199999987213431e-10) - 1.3862944 * jax.random.uniform(streams_of[18], (D, FF), jnp.float32) ** shard_levels(streams_of[18], (D, FF), ((0, 32),), -0.2, 0.2)), 7.999999968033578e-11, 3.199999987213431e-10)
    w_down = noise(streams_of[19], (FF, D), FF ** -0.5, 0.109375, ((0, 32),), jnp.float32)
    moment_down = noise(streams_of[20], (FF, D), 0.00003, 0.0004272461, ((0, 32),), jnp.float32)
    square_down = jnp.clip(jnp.exp(math.log(3.199999987213431e-10) - 1.3862944 * jax.random.uniform(streams_of[21], (FF, D), jnp.float32) ** shard_levels(streams_of[21], (FF, D), ((0, 32),), -0.2, 0.2)), 7.999999968033578e-11, 3.199999987213431e-10)
    gains = draw_gains(jax.random.fold_in(streams_of[25], 71), 0)
    moment_gains = noise(streams_of[23], (2, D), 0.00006, 0.0008544922, ((1, 32),), jnp.float32)
    square_gains = jnp.clip(jnp.exp(math.log(8.000000106811456e-10) - 1.3862944 * jax.random.uniform(streams_of[24], (2, D), jnp.float32) ** shard_levels(streams_of[24], (2, D), ((1, 32),), -0.2, 0.2)), 2.000000026702864e-10, 8.000000106811456e-10)
    return {"tokens": tokens, "cotangent": cotangent, "cache_keys": cache_keys, "cache_values": cache_values, "neighbours": neighbours, "partner": partner, "has_memory": has_memory, "w_heads": w_heads, "moment_heads": moment_heads, "square_heads": square_heads, "w_merge": w_merge, "moment_merge": moment_merge, "square_merge": square_merge, "w_gate": w_gate, "moment_gate": moment_gate, "square_gate": square_gate, "w_up": w_up, "moment_up": moment_up, "square_up": square_up, "w_down": w_down, "moment_down": moment_down, "square_down": square_down, "gains": gains, "moment_gains": moment_gains, "square_gains": square_gains}


NORM_EPS = 1e-06
BETA_ONE = 0.9
BETA_TWO = 0.999
ADAM_EPS = 1e-06
DECAY = 0.01
RATE = 0.5
CLIP = 1.0
HIGH = lax.Precision.HIGHEST

@jax.custom_vjp
def low(v):
    return lax.optimization_barrier(v.astype(jnp.bfloat16)).astype(jnp.float32)

@jax.custom_vjp
def low_back(v):
    return v

def low_keep(v):
    return (low(v), None)

def low_pass(kept, grad):
    return (grad,)

def back_keep(v):
    return (v, None)

def back_low(kept, grad):
    return (low(grad),)
low.defvjp(low_keep, low_pass)
low_back.defvjp(back_keep, back_low)

def rms_scale(values, gain_row):
    return values * lax.rsqrt(lax.optimization_barrier(jnp.mean(values * values, axis=-1, keepdims=True)) + NORM_EPS) * gain_row

def angles(positions, half_size):
    frequency = jnp.exp(-jnp.log(10000.0) * jnp.arange(half_size, dtype=jnp.float32) / half_size)
    angle_grid = positions.astype(jnp.float32)[:, None] * frequency[None, :]
    return (jnp.cos(angle_grid)[:, None, :], jnp.sin(angle_grid)[:, None, :])

def rotate(values, cosine_table, sine_table):
    half_size = values.shape[-1] // 2
    first_half = values[..., :half_size]
    second_half = values[..., half_size:]
    return jnp.concatenate([first_half * cosine_table - second_half * sine_table, second_half * cosine_table + first_half * sine_table], axis=-1)

def document(inputs, w_heads, w_merge, w_gate, w_up, w_down, gains, memory_keys, memory_values, allowed):
    gain_low = low(gains)
    normed_one = low(rms_scale(inputs, gain_low[0]))
    projected = low_back(jnp.dot(normed_one, low(w_heads), precision=HIGH))
    head_shape = (LEN, HEADS, HEAD_DIM)
    query_raw = projected[:, :D].reshape(head_shape)
    key_raw = projected[:, D:2 * D].reshape(head_shape)
    value_raw = projected[:, 2 * D:].reshape(head_shape)
    cosine_table, sine_table = angles(jnp.arange(LEN, dtype=jnp.int32), HEAD_DIM // 2)
    query_local = low(rotate(query_raw, cosine_table, sine_table))
    key_local = low(rotate(key_raw, cosine_table, sine_table))
    value_local = low(value_raw)
    query_memory = low(query_raw)
    score_scale = HEAD_DIM ** (-0.5)
    span_rows = min(512, LEN)

    def attend(block_index):
        block_start = block_index * span_rows
        query_one = lax.dynamic_slice_in_dim(query_local, block_start, span_rows, 0)
        query_two = lax.dynamic_slice_in_dim(query_memory, block_start, span_rows, 0)
        chosen = lax.dynamic_slice_in_dim(allowed, block_start, span_rows, 0)
        local_scores = jnp.einsum('qhe,khe->hqk', query_one, key_local, precision=HIGH) * score_scale
        causal = (block_start + jnp.arange(span_rows, dtype=jnp.int32))[:, None] >= jnp.arange(LEN, dtype=jnp.int32)[None, :]
        local_scores = jnp.where(causal[None], local_scores, -jnp.inf)
        remote = jnp.einsum('qhe,khe->hqk', query_two, memory_keys, precision=HIGH) * score_scale
        remote = jnp.where(chosen[None], remote, -jnp.inf)
        scores = low_back(jnp.concatenate([local_scores, remote], axis=-1))
        highest = lax.optimization_barrier(jnp.max(scores, axis=-1, keepdims=True))
        expo = jnp.exp(scores - highest)
        probability = low(expo / lax.optimization_barrier(jnp.sum(expo, axis=-1, keepdims=True)))
        return jnp.einsum('hqk,khe->qhe', probability[..., :LEN], value_local, precision=HIGH) + jnp.einsum('hqk,khe->qhe', probability[..., LEN:], memory_values, precision=HIGH)
    attended = lax.map(jax.checkpoint(attend), jnp.arange(LEN // span_rows, dtype=jnp.int32))
    blended = low(low_back(attended.reshape(LEN, D)))
    middle = inputs + low_back(jnp.dot(blended, low(w_merge), precision=HIGH))
    normed_two = low(rms_scale(middle, gain_low[1]))
    gate_raw = low_back(jnp.dot(normed_two, low(w_gate), precision=HIGH))
    up_raw = low_back(jnp.dot(normed_two, low(w_up), precision=HIGH))
    active = low(gate_raw * jax.nn.sigmoid(gate_raw) * up_raw)
    return middle + low_back(jnp.dot(active, low(w_down), precision=HIGH))

def reference(tokens, cotangent, cache_keys, cache_values, neighbours, partner, has_memory, w_heads, moment_heads, square_heads, w_merge, moment_merge, square_merge, w_gate, moment_gate, square_gate, w_up, moment_up, square_up, w_down, moment_down, square_down, gains, moment_gains, square_gains):
    masters = (w_heads, w_merge, w_gate, w_up, w_down, gains)
    moments = (moment_heads, moment_merge, moment_gate, moment_up, moment_down, moment_gains)
    squares = (square_heads, square_merge, square_gate, square_up, square_down, square_gains)
    decays = (DECAY, DECAY, DECAY, DECAY, DECAY, 0.0)

    def one_document(totals, doc_number):
        inputs = tokens[doc_number].astype(jnp.float32)
        mate_doc = partner[doc_number]
        memory_keys = jnp.concatenate([cache_keys[doc_number], cache_keys[mate_doc]], axis=0)
        memory_keys = memory_keys.astype(jnp.float32).reshape(2 * MEM, HEADS, HEAD_DIM)
        memory_values = jnp.concatenate([cache_values[doc_number], cache_values[mate_doc]], axis=0)
        memory_values = memory_values.astype(jnp.float32).reshape(2 * MEM, HEADS, HEAD_DIM)
        row_ids = jnp.arange(LEN, dtype=jnp.int32)[:, None]
        picked_keys = jnp.zeros((LEN, 2 * MEM), jnp.bool_).at[row_ids, neighbours[doc_number]].set(True)
        allowed = picked_keys & (has_memory[doc_number] > 0)

        def forward(inputs, w_one, w_two, w_three, w_four, w_five, gain_rows):
            return document(inputs, w_one, w_two, w_three, w_four, w_five, gain_rows, memory_keys, memory_values, allowed)
        result, pullback = jax.vjp(forward, inputs, *masters)
        pulled = pullback(cotangent[doc_number].astype(jnp.float32))
        totals = tuple((summed + fresh for summed, fresh in zip(totals, pulled[1:])))
        return (totals, (result.astype(jnp.bfloat16), pulled[0]))
    zero_grads = tuple((jnp.zeros(member.shape, jnp.float32) for member in masters))
    reduced, (activations, input_grad) = lax.scan(one_document, zero_grads, jnp.arange(DOCS, dtype=jnp.int32))
    grad_norm = jnp.sqrt(jnp.sum(jnp.stack([jnp.sum(member * member) for member in reduced])))
    factor = CLIP / jnp.maximum(grad_norm, CLIP)
    fix_one = 1.0 - BETA_ONE ** STEP
    fix_two = 1.0 - BETA_TWO ** STEP
    new_moments = []
    new_squares = []
    directions = []
    for master, moment, square, gradient, decay_rate in zip(masters, moments, squares, reduced, decays):
        clipped = factor * gradient
        moment_new = BETA_ONE * moment + (1.0 - BETA_ONE) * clipped
        square_new = BETA_TWO * square + (1.0 - BETA_TWO) * clipped * clipped
        direction = moment_new / fix_one / (jnp.sqrt(square_new / fix_two) + ADAM_EPS) + decay_rate * master
        new_moments.append(moment_new)
        new_squares.append(square_new)
        directions.append(direction)
    weight_norm = jnp.sqrt(jnp.stack([jnp.sum(member * member) for member in masters]))
    update_norm = jnp.sqrt(jnp.stack([jnp.sum(member * member) for member in directions]))
    trust = weight_norm / update_norm
    new_weights = [master - RATE * trust[place] * directions[place] for place, master in enumerate(masters)]
    layer_norms = jnp.stack([weight_norm, update_norm])
    return (activations, input_grad, new_moments[0], new_squares[0], new_weights[0], new_moments[1], new_squares[1], new_weights[1], new_moments[2], new_squares[2], new_weights[2], new_moments[3], new_squares[3], new_weights[3], new_moments[4], new_squares[4], new_weights[4], new_moments[5], new_squares[5], new_weights[5], grad_norm, layer_norms)
```

```python
import functools
import math

import jax
import jax.numpy as jnp
from jax import lax
from jax.experimental import pallas as pl
from jax.experimental.pallas import tpu as pltpu
from jax.sharding import PartitionSpec as P

HEADS = 8
HEAD_DIM = 128
STEP = 10
NORM_EPS = 1e-06
BETA_ONE = 0.9
BETA_TWO = 0.999
ADAM_EPS = 1e-06
DECAY = 0.01
RATE = 0.5
CLIP = 1.0
LANES = 128
LOG2E = math.log2(math.e)
SCALE = HEAD_DIM ** (-0.5)
BF = jnp.bfloat16
F32 = jnp.float32
VMEM_LIMIT = 56 * 1024 * 1024


def seq_shape():
    count = lax.axis_size("seq")
    cores = 2 if count % 2 == 0 else 1
    return count // cores, cores


def docs_shape():
    count = lax.axis_size("docs")
    nx = 1 << ((count.bit_length() - 1) // 2)
    while count % nx:
        nx //= 2
    return count // nx, nx


def send_seq(x, dy, dc):
    ny, nc = seq_shape()
    pairs = [
        (y * nc + c, (y + dy) % ny * nc + (c + dc) % nc) for y in range(ny) for c in range(nc)
    ]
    return lax.ppermute(x, "seq", pairs)


def send_x(x, dx):
    nz, nx = docs_shape()
    pairs = [(z * nx + i, z * nx + (i + dx) % nx) for z in range(nz) for i in range(nx)]
    return lax.ppermute(x, "docs", pairs)


def send_z(x, step, senders):
    nz, nx = docs_shape()
    pairs = [(z * nx + i, (z + step) * nx + i) for z in senders for i in range(nx)]
    return lax.ppermute(x, "docs", pairs)


def put(buffer, block, place):
    starts = list(place) + [0] * (buffer.ndim - len(place))
    block = block.reshape((1,) * (buffer.ndim - block.ndim) + block.shape)
    return lax.dynamic_update_slice(buffer, block, starts)


def seq_gather(block):
    ny, nc = seq_shape()
    index = lax.axis_index("seq")
    y, c = index // nc, index % nc
    column = jnp.zeros((ny,) + block.shape, block.dtype)
    column = put(column, block, [y])
    for dy in range(1, ny):
        column = put(column, send_seq(block, dy, 0), [(y - dy) % ny])
    whole = jnp.zeros((ny, nc) + block.shape, block.dtype)
    whole = lax.dynamic_update_slice(whole, column[:, None], (0, c, 0, 0))
    for dc in range(1, nc):
        other = send_seq(column, 0, dc)
        whole = lax.dynamic_update_slice(whole, other[:, None], (0, (c - dc) % nc, 0, 0))
    return whole.reshape((ny * nc * block.shape[0],) + block.shape[1:])


def seq_reduce(partial):
    ny, nc = seq_shape()
    index = lax.axis_index("seq")
    y, c = index // nc, index % nc
    rows = partial.shape[0] // (ny * nc)
    blocks = partial.reshape(ny, nc, rows, partial.shape[1])
    column = lax.dynamic_index_in_dim(blocks, c, 1, False)
    for dc in range(1, nc):
        away = lax.dynamic_index_in_dim(blocks, (c + dc) % nc, 1, False).astype(BF)
        column = column + send_seq(away, 0, dc).astype(F32)
    total = lax.dynamic_index_in_dim(column, y, 0, False)
    for dy in range(1, ny):
        away = lax.dynamic_index_in_dim(column, (y + dy) % ny, 0, False).astype(BF)
        total = total + send_seq(away, dy, 0).astype(F32)
    return total


def seq_swap(blocks):
    ny, nc = seq_shape()
    index = lax.axis_index("seq")
    y, c = index // nc, index % nc
    out = jnp.zeros_like(blocks)
    out = put(out, lax.dynamic_index_in_dim(blocks, index, 0, False), [index])
    for dy in range(ny):
        for dc in range(nc):
            if dy == 0 and dc == 0:
                continue
            there = (y + dy) % ny * nc + (c + dc) % nc
            here = (y - dy) % ny * nc + (c - dc) % nc
            away = lax.dynamic_index_in_dim(blocks, there, 0, False)
            out = put(out, send_seq(away, dy, dc), [here])
    return out


def docs_gather(block):
    nz, nx = docs_shape()
    index = lax.axis_index("docs")
    z, x = index // nx, index % nx
    ups, downs = [block], [block]
    for step in range(1, nz):
        ups.append(send_z(ups[-1], 1, range(step - 1, nz - 1)))
        downs.append(send_z(downs[-1], -1, range(1, nz - step + 1)))
    column = jnp.zeros((nz,) + block.shape, block.dtype)
    column = put(column, block, [z])
    for step in range(1, nz):
        arrived = jnp.where(z >= step, ups[step], downs[nz - step])
        column = put(column, arrived, [(z - step) % nz])
    whole = jnp.zeros((nz, nx) + block.shape, block.dtype)
    whole = lax.dynamic_update_slice(whole, column[:, None], (0, x, 0, 0))
    for dx in range(1, nx):
        other = send_x(column, dx)
        whole = lax.dynamic_update_slice(whole, other[:, None], (0, (x - dx) % nx, 0, 0))
    return whole.reshape((nz * nx,) + block.shape)


def docs_reduce(blocks):
    nz, nx = docs_shape()
    index = lax.axis_index("docs")
    z, x = index // nx, index % nx
    grid = blocks.reshape((nz, nx) + blocks.shape[1:])
    column = lax.dynamic_index_in_dim(grid, x, 1, False).astype(F32)
    for dx in range(1, nx):
        away = lax.dynamic_index_in_dim(grid, (x + dx) % nx, 1, False).astype(BF)
        column = column + send_x(away, dx).astype(F32)
    total = lax.dynamic_index_in_dim(column, z, 0, False)
    for sign in (1, -1):
        carry = None
        for step in range(nz - 1, 0, -1):
            place = jnp.clip(z + sign * step, 0, nz - 1)
            value = lax.dynamic_index_in_dim(column, place, 0, False)
            if carry is not None:
                value = value + carry.astype(F32)
            senders = range(nz - step) if sign > 0 else range(step, nz)
            carry = send_z(value.astype(BF), sign, senders)
        if carry is not None:
            total = total + carry.astype(F32)
    return total


def sum_everywhere(values):
    for axis in ("seq", "docs"):
        count = lax.axis_size(axis)
        if count & (count - 1):
            values = lax.psum(values, axis)
            continue
        reach = 1
        while reach < count:
            values = values + lax.ppermute(values, axis, [(i, i ^ reach) for i in range(count)])
            reach *= 2
    return values


def dot(a, b):
    return lax.dot_general(a, b, (((1,), (0,)), ((), ())), preferred_element_type=F32)


def dot_nt(a, b):
    return lax.dot_general(a, b, (((1,), (1,)), ((), ())), preferred_element_type=F32)


def dot_tn(a, b):
    return lax.dot_general(a, b, (((0,), (0,)), ((), ())), preferred_element_type=F32)


def params():
    return pltpu.CompilerParams(vmem_limit_bytes=VMEM_LIMIT)


def rows_of(rows, cols):
    return pl.BlockSpec((rows, cols), lambda i: (i, 0))


def all_of(rows, cols):
    return pl.BlockSpec((rows, cols), lambda i: (0, 0))


def project_kernel(heads, x, gain, weight, cosine, sine, normed, ql, qm, kl, vl):
    values = x[...].astype(F32)
    scale = lax.rsqrt(jnp.mean(values * values, axis=-1, keepdims=True) + NORM_EPS)
    low = (values * scale * gain[...]).astype(BF)
    normed[...] = low
    out = dot(low, weight[...])
    width = heads * HEAD_DIM
    cos, sin = cosine[...], sine[...]
    for h in range(heads):
        part = slice(h * HEAD_DIM, (h + 1) * HEAD_DIM)
        q = out[:, h * HEAD_DIM : (h + 1) * HEAD_DIM]
        k = out[:, width + h * HEAD_DIM : width + (h + 1) * HEAD_DIM]
        qm[:, part] = q.astype(BF)
        ql[:, part] = (q * cos + pltpu.roll(q, HEAD_DIM // 2, 1) * sin).astype(BF)
        kl[:, part] = (k * cos + pltpu.roll(k, HEAD_DIM // 2, 1) * sin).astype(BF)
    vl[...] = out[:, 2 * width : 3 * width].astype(BF)


def project(x, gain, weight, cosine, sine, heads):
    length, width = x.shape
    span = min(256, length)
    cols = heads * HEAD_DIM
    low = jax.ShapeDtypeStruct((length, cols), BF)
    return pl.pallas_call(
        functools.partial(project_kernel, heads),
        grid=(length // span,),
        in_specs=[
            rows_of(span, width),
            all_of(1, width),
            all_of(width, 3 * cols),
            rows_of(span, HEAD_DIM),
            rows_of(span, HEAD_DIM),
        ],
        out_specs=[rows_of(span, width)] + [rows_of(span, cols)] * 4,
        out_shape=[jax.ShapeDtypeStruct((length, width), BF)] + [low] * 4,
        compiler_params=params(),
        name="project",
    )(x, gain, weight, cosine, sine)


def causal(span, length):
    row = pl.program_id(0) * span + lax.broadcasted_iota(jnp.int32, (span, length), 0)
    return lax.broadcasted_iota(jnp.int32, (span, length), 1) <= row


def allowed(words, chunk, chunk_keys):
    tiles = chunk_keys // LANES
    parts = []
    for tile in range(tiles):
        bit = chunk * tiles + tile
        mask = (1 << bit) if bit < 31 else -(1 << 31)
        parts.append((words & jnp.int32(mask)) != 0)
    return parts


def select_tiles(parts, values, other):
    cut = [
        jnp.where(part, values[:, t * LANES : (t + 1) * LANES], other)
        for t, part in enumerate(parts)
    ]
    return jnp.concatenate(cut, axis=1)


def attend_kernel(heads, chunk_keys, flag, ql, qm, kl, vl, words, kv, out, low, lse, high, total):
    span = ql.shape[0]
    length = kl.shape[0]
    width = heads * HEAD_DIM
    factor = SCALE * LOG2E
    seen = causal(span, length)
    for h in range(heads):
        part = slice(h * HEAD_DIM, (h + 1) * HEAD_DIM)
        scores = dot_nt(ql[:, part], kl[:, part]) * factor
        scores = jnp.where(seen, scores, -jnp.inf)
        top = jnp.max(scores, axis=1, keepdims=True)
        expo = jnp.exp2(scores - top)
        high[:, h : h + 1] = top
        total[:, h : h + 1] = jnp.sum(expo, axis=1, keepdims=True)
        out[:, part] = dot(expo.astype(BF), vl[:, part])

    @pl.when(flag[0] > 0)
    def _():
        bits = words[...]
        count = kv.shape[0] // chunk_keys
        state = [
            (high[:, h : h + 1], total[:, h : h + 1], out[:, h * HEAD_DIM : (h + 1) * HEAD_DIM])
            for h in range(heads)
        ]
        for chunk in range(count):
            here = slice(chunk * chunk_keys, (chunk + 1) * chunk_keys)
            parts = allowed(bits, chunk, chunk_keys)
            for h in range(heads):
                part = slice(h * HEAD_DIM, (h + 1) * HEAD_DIM)
                top, weight, sums = state[h]
                scores = dot_nt(qm[:, part], kv[here, part]) * factor
                scores = select_tiles(parts, scores, -jnp.inf)
                new_top = jnp.maximum(top, jnp.max(scores, axis=1, keepdims=True))
                shrink = jnp.exp2(top - new_top)
                expo = jnp.exp2(scores - new_top)
                weight = weight * shrink + jnp.sum(expo, axis=1, keepdims=True)
                value = kv[here, width + h * HEAD_DIM : width + (h + 1) * HEAD_DIM]
                sums = sums * shrink + dot(expo.astype(BF), value)
                state[h] = (new_top, weight, sums)
        for h in range(heads):
            high[:, h : h + 1], total[:, h : h + 1] = state[h][0], state[h][1]
            out[:, h * HEAD_DIM : (h + 1) * HEAD_DIM] = state[h][2]

    for h in range(heads):
        part = slice(h * HEAD_DIM, (h + 1) * HEAD_DIM)
        sums = total[:, h : h + 1]
        values = out[:, part] / sums
        out[:, part] = values
        low[:, part] = values.astype(BF)
        lse[:, h : h + 1] = high[:, h : h + 1] + jnp.log2(sums)


def attend(flag, ql, qm, kl, vl, words, kv, heads):
    length, width = ql.shape
    span = min(256, length)
    keys = kv.shape[0]
    return pl.pallas_call(
        functools.partial(attend_kernel, heads, min(1024, keys)),
        grid=(length // span,),
        in_specs=[
            pl.BlockSpec(memory_space=pltpu.SMEM),
            rows_of(span, width),
            rows_of(span, width),
            all_of(length, width),
            all_of(length, width),
            rows_of(span, LANES),
            all_of(keys, 2 * width),
        ],
        out_specs=[rows_of(span, width), rows_of(span, width), rows_of(span, LANES)],
        out_shape=[
            jax.ShapeDtypeStruct((length, width), F32),
            jax.ShapeDtypeStruct((length, width), BF),
            jax.ShapeDtypeStruct((length, LANES), F32),
        ],
        scratch_shapes=[pltpu.VMEM((span, LANES), F32), pltpu.VMEM((span, LANES), F32)],
        compiler_params=params(),
        name="attend",
    )(flag, ql, qm, kl, vl, words, kv)


def attend_back_kernel(
    heads, chunk_keys, flag, ql, qm, kl, vl, words, kv, att, go, lse, cosq, sinq, cosk, sink,
    gq, gk, gv, sum_k, sum_v, sum_q,
):
    span = ql.shape[0]
    length = kl.shape[0]
    width = heads * HEAD_DIM
    factor = SCALE * LOG2E
    step = pl.program_id(0)
    last = pl.num_programs(0) - 1
    seen = causal(span, length)

    @pl.when(step == 0)
    def _():
        sum_k[...] = jnp.zeros_like(sum_k)
        sum_v[...] = jnp.zeros_like(sum_v)

    deltas = []
    for h in range(heads):
        part = slice(h * HEAD_DIM, (h + 1) * HEAD_DIM)
        grad = go[:, part]
        delta = jnp.sum(grad.astype(F32) * att[:, part], axis=1, keepdims=True)
        deltas.append(delta)
        query = ql[:, part]
        scores = dot_nt(query, kl[:, part]) * factor
        prob = jnp.where(seen, jnp.exp2(scores - lse[:, h : h + 1]), 0.0)
        grad_prob = dot_nt(grad, vl[:, part])
        grad_scores = (prob * (grad_prob - delta)).astype(BF)
        sum_v[:, part] += dot_tn(prob.astype(BF), grad)
        sum_k[:, part] += dot_tn(grad_scores, query)
        back = dot(grad_scores, kl[:, part]) * SCALE
        back = back * cosq[...] - pltpu.roll(back, HEAD_DIM // 2, 1) * sinq[...]
        sum_q[:, part] = back

    @pl.when(flag[0] > 0)
    def _():
        bits = words[...]
        count = kv.shape[0] // chunk_keys
        sums = [None] * heads
        for chunk in range(count):
            here = slice(chunk * chunk_keys, (chunk + 1) * chunk_keys)
            parts = allowed(bits, chunk, chunk_keys)
            for h in range(heads):
                part = slice(h * HEAD_DIM, (h + 1) * HEAD_DIM)
                key = kv[here, part]
                scores = dot_nt(qm[:, part], key) * factor
                prob = select_tiles(parts, jnp.exp2(scores - lse[:, h : h + 1]), 0.0)
                value = kv[here, width + h * HEAD_DIM : width + (h + 1) * HEAD_DIM]
                grad_prob = dot_nt(go[:, part], value)
                grad_scores = (prob * (grad_prob - deltas[h])).astype(BF)
                fresh = dot(grad_scores, key)
                sums[h] = fresh if sums[h] is None else sums[h] + fresh
        for h in range(heads):
            sum_q[:, h * HEAD_DIM : (h + 1) * HEAD_DIM] += sums[h] * SCALE

    gq[...] = sum_q[...].astype(BF)

    @pl.when(step == last)
    def _():
        gv[...] = sum_v[...].astype(BF)
        for h in range(heads):
            part = slice(h * HEAD_DIM, (h + 1) * HEAD_DIM)
            back = sum_k[:, part] * SCALE
            back = back * cosk[...] - pltpu.roll(back, HEAD_DIM // 2, 1) * sink[...]
            gk[:, part] = back.astype(BF)


def attend_back(flag, ql, qm, kl, vl, words, kv, att, go, lse, cosine, sine, heads):
    length, width = ql.shape
    span = min(256, length)
    keys = kv.shape[0]
    low = jax.ShapeDtypeStruct((length, width), BF)
    return pl.pallas_call(
        functools.partial(attend_back_kernel, heads, min(1024, keys)),
        grid=(length // span,),
        in_specs=[
            pl.BlockSpec(memory_space=pltpu.SMEM),
            rows_of(span, width),
            rows_of(span, width),
            all_of(length, width),
            all_of(length, width),
            rows_of(span, LANES),
            all_of(keys, 2 * width),
            rows_of(span, width),
            rows_of(span, width),
            rows_of(span, LANES),
            rows_of(span, HEAD_DIM),
            rows_of(span, HEAD_DIM),
            all_of(length, HEAD_DIM),
            all_of(length, HEAD_DIM),
        ],
        out_specs=[rows_of(span, width), all_of(length, width), all_of(length, width)],
        out_shape=[low] * 3,
        scratch_shapes=[
            pltpu.VMEM((length, width), F32),
            pltpu.VMEM((length, width), F32),
            pltpu.VMEM((span, width), F32),
        ],
        compiler_params=params(),
        name="attend_back",
    )(flag, ql, qm, kl, vl, words, kv, att, go, lse, cosine, sine, cosine, sine)


def norm_rows(values):
    row_scale = lax.rsqrt(jnp.mean(values * values, axis=-1, keepdims=True) + NORM_EPS)
    return (values * row_scale, row_scale)


def norm_back(grad_normed, unit_rows, row_scale, gain_row):
    weighted = grad_normed * gain_row
    inner = jnp.mean(weighted * unit_rows, axis=-1, keepdims=True)
    return row_scale * (weighted - unit_rows * inner)


def rotation(length):
    half = HEAD_DIM // 2
    frequency = jnp.exp(-jnp.log(10000.0) * jnp.arange(half, dtype=F32) / half)
    grid = jnp.arange(length, dtype=F32)[:, None] * frequency[None, :]
    cos, sin = jnp.cos(grid), jnp.sin(grid)
    return jnp.concatenate([cos, cos], 1), jnp.concatenate([-sin, sin], 1)


def mask_words(neighbours, per_device):
    memory = per_device * lax.axis_size("docs") * lax.axis_size("seq")
    doc, slot = neighbours // memory, neighbours % memory
    source, row = slot // per_device, slot % per_device
    place = source * (2 * per_device) + doc * per_device + row
    bit = jnp.left_shift(jnp.int32(1), place // LANES)
    lane = jnp.arange(LANES, dtype=jnp.int32)
    hits = jnp.where((place % LANES)[:, :, None] == lane, bit[:, :, None], 0)
    return lax.reduce(hits, jnp.int32(0), lax.bitwise_or, (1,))


def shards(
    tokens, cotangent, cache_keys, cache_values, neighbours, partner, has_memory,
    w_heads, moment_heads, square_heads, w_merge, moment_merge, square_merge,
    w_gate, moment_gate, square_gate, w_up, moment_up, square_up,
    w_down, moment_down, square_down, gains, moment_gains, square_gains,
):
    _, rows, width = tokens.shape
    seq_count = lax.axis_size("seq")
    docs_count = lax.axis_size("docs")
    devices = seq_count * docs_count
    seq_index = lax.axis_index("seq")
    doc_index = lax.axis_index("docs")
    length = rows * seq_count
    heads = HEADS // seq_count
    cols = heads * HEAD_DIM
    weight_rows = w_heads.shape[0]
    down_rows = w_down.shape[0]
    inner = w_gate.shape[1] // seq_count
    inner_pad = -(-inner // LANES) * LANES
    per_device = cache_keys.shape[1]
    masters = (w_heads, w_merge, w_gate, w_up, w_down, gains)
    moments = (moment_heads, moment_merge, moment_gate, moment_up, moment_down, moment_gains)
    squares = (square_heads, square_merge, square_gate, square_up, square_down, square_gains)
    decays = (DECAY, DECAY, DECAY, DECAY, DECAY, 0.0)
    lows = [member.astype(BF) for member in masters]

    pair = jnp.stack([cache_keys, cache_values], axis=2)
    pair = jnp.stack([pair, jnp.take(pair, partner, axis=0)], axis=1)
    pair = pair.reshape(docs_count, 2 * per_device, 2, seq_count, cols)
    pair = pair.transpose(0, 3, 1, 2, 4).reshape(devices, 2 * per_device, 2 * cols)
    memory = lax.all_to_all(pair, ("docs", "seq"), split_axis=0, concat_axis=0, tiled=True)
    memory = memory.reshape(devices * 2 * per_device, 2 * cols)
    flag = jnp.take(has_memory, doc_index[None])

    def columns(member):
        split = member.reshape(weight_rows, docs_count, seq_count, down_rows)
        split = split.transpose(2, 0, 1, 3).reshape(seq_count, weight_rows, inner)
        return jnp.pad(split, ((0, 0), (0, 0), (0, inner_pad - inner)))

    by_head = lows[0].reshape(weight_rows, 3, seq_count, cols).transpose(2, 0, 1, 3)
    by_head = by_head.reshape(seq_count, weight_rows, 3 * cols)
    gain_cols = jnp.pad(lows[5].T, ((0, 0), (0, LANES - 2)))
    gain_cols = jnp.broadcast_to(gain_cols[None], (seq_count, weight_rows, LANES))
    first = seq_swap(jnp.concatenate([by_head, gain_cols], axis=2))
    first = docs_gather(first.reshape(seq_count * weight_rows, 3 * cols + LANES))
    first = first.reshape(width, 3 * cols + LANES)
    heads_here = first[:, : 3 * cols]
    gain_one = first[:, 3 * cols].astype(F32)[None, :]
    gain_two = first[:, 3 * cols + 1].astype(F32)[None, :]

    x_low = seq_gather(tokens[0])
    words = mask_words(seq_gather(neighbours[0]), per_device)
    cosine, sine = rotation(length)
    normed_one, query_local, query_memory, key_local, value_local = project(
        x_low, gain_one, heads_here, cosine, sine, heads
    )

    second = docs_gather(jnp.concatenate([lows[1], lows[4]], axis=0))
    merge_here = second[:, :weight_rows].reshape(docs_count * weight_rows, width)
    merge_full = seq_gather(merge_here).reshape(seq_count, docs_count, weight_rows, width)
    merge_full = merge_full.transpose(1, 0, 2, 3).reshape(width, width)
    down_here = second[:, weight_rows:].reshape(inner, width)
    down_here = jnp.pad(down_here, ((0, inner_pad - inner), (0, 0)))
    third = seq_swap(jnp.concatenate([columns(lows[2]), columns(lows[3])], axis=2))
    third = docs_gather(third.reshape(seq_count * weight_rows, 2 * inner_pad))
    gate_up = third.reshape(width, 2 * inner_pad)
    grad_low = seq_gather(cotangent[0])

    attended, blended_here, lse = attend(
        flag, query_local, query_memory, key_local, value_local, words, memory, heads
    )

    def mine(member):
        return lax.dynamic_slice_in_dim(member, seq_index * rows, rows, 0)

    blended = seq_gather(blended_here)
    blended = blended.reshape(seq_count, length, cols).transpose(1, 0, 2).reshape(length, width)
    middle = x_low.astype(F32) + jnp.dot(blended, merge_full, preferred_element_type=F32)
    unit_two, _ = norm_rows(middle)
    normed_two = (unit_two * gain_two).astype(BF)
    raw = jnp.dot(normed_two, gate_up, preferred_element_type=F32)
    gate_raw, up_raw = raw[:, :inner_pad], raw[:, inner_pad:]
    sigmoid_gate = jax.nn.sigmoid(gate_raw)
    silu_gate = gate_raw * sigmoid_gate
    active = (silu_gate * up_raw).astype(BF)
    grad_active = dot_nt(grad_low, down_here)
    grad_gate = grad_active * up_raw * sigmoid_gate * (1.0 + gate_raw * (1.0 - sigmoid_gate))
    grad_up = grad_active * silu_gate
    grad_raw = jnp.concatenate([grad_gate.astype(BF), grad_up.astype(BF)], axis=1)

    grad_normed_two = seq_reduce(dot_nt(grad_raw, gate_up))
    middle_mine = mine(middle)
    unit_mine, scale_mine = norm_rows(middle_mine)
    grad_middle = cotangent[0].astype(F32) + norm_back(
        grad_normed_two, unit_mine, scale_mine, gain_two
    )
    grad_branch = seq_gather(grad_middle.astype(BF))
    merge_rows = lax.dynamic_slice_in_dim(merge_full, seq_index * cols, cols, 0)
    grad_attended = dot_nt(grad_branch, merge_rows).astype(BF)

    g_raw = dot_tn(normed_two, grad_raw).astype(BF)
    g_raw = lax.psum_scatter(g_raw, "docs", scatter_dimension=0, tiled=True)
    g_down = dot_tn(active, grad_low)[:inner].astype(BF)
    g_down = lax.psum_scatter(g_down, "docs", scatter_dimension=0, tiled=True)
    g_merge = dot_tn(blended, grad_branch).reshape(docs_count, seq_count, weight_rows, width)
    g_merge = lax.dynamic_index_in_dim(g_merge, seq_index, 1, False).astype(BF)
    g_merge = lax.psum_scatter(
        g_merge.reshape(docs_count * weight_rows, width), "docs", scatter_dimension=0, tiled=True
    )

    down_out = jnp.dot(active, down_here, preferred_element_type=F32)
    activations = (middle_mine + seq_reduce(down_out)).astype(BF)[None]

    grad_q, grad_k, grad_v = attend_back(
        flag, query_local, query_memory, key_local, value_local, words, memory,
        attended, grad_attended, lse, cosine, sine, heads,
    )
    grad_projected = jnp.concatenate([grad_q, grad_k, grad_v], axis=1)
    g_heads = dot_tn(normed_one, grad_projected)
    g_heads = docs_reduce(g_heads.reshape(docs_count, width // docs_count, 3 * cols))
    grad_normed_one = seq_reduce(dot_nt(grad_projected, heads_here))
    unit_one, scale_one = norm_rows(tokens[0].astype(F32))
    input_grad = grad_middle + norm_back(grad_normed_one, unit_one, scale_one, gain_one)
    input_grad = input_grad[None]

    def own_rows(member):
        return seq_swap(member.astype(BF).reshape(seq_count, weight_rows, member.shape[1]))

    g_heads = own_rows(g_heads).reshape(seq_count, weight_rows, 3, cols)
    g_heads = g_heads.transpose(1, 2, 0, 3).reshape(weight_rows, 3 * width).astype(F32)
    g_raw = own_rows(g_raw).reshape(seq_count, weight_rows, 2, inner_pad)[..., :inner]
    g_raw = g_raw.reshape(seq_count, weight_rows, 2, docs_count, down_rows)
    g_raw = g_raw.transpose(2, 1, 3, 0, 4).reshape(2, weight_rows, inner * seq_count).astype(F32)
    g_gate, g_up = g_raw[0], g_raw[1]
    gain_rows = [lows[5][0].astype(F32), lows[5][1].astype(F32)]
    g_gain_one = jnp.sum(g_heads * lows[0].astype(F32), axis=1) / gain_rows[0]
    g_gain_two = (
        jnp.sum(g_gate * lows[2].astype(F32) + g_up * lows[3].astype(F32), axis=1) / gain_rows[1]
    )
    reduced = (
        g_heads,
        g_merge.astype(F32),
        g_gate,
        g_up,
        g_down.astype(F32),
        jnp.stack([g_gain_one, g_gain_two]),
    )

    weight_local = jnp.stack([jnp.sum(member * member) for member in masters])
    grad_local = sum(jnp.sum(member * member) for member in reduced)
    totals = sum_everywhere(jnp.concatenate([grad_local[None], weight_local]))
    grad_norm = jnp.sqrt(totals[0])
    factor = CLIP / jnp.maximum(grad_norm, CLIP)
    fix_one = 1.0 - BETA_ONE**STEP
    fix_two = 1.0 - BETA_TWO**STEP
    new_moments = []
    new_squares = []
    directions = []
    for master, moment, square, gradient, decay_rate in zip(
        masters, moments, squares, reduced, decays
    ):
        clipped = factor * gradient
        moment_new = BETA_ONE * moment + (1.0 - BETA_ONE) * clipped
        square_new = BETA_TWO * square + (1.0 - BETA_TWO) * clipped * clipped
        direction = (
            moment_new / fix_one / (jnp.sqrt(square_new / fix_two) + ADAM_EPS) + decay_rate * master
        )
        new_moments.append(moment_new)
        new_squares.append(square_new)
        directions.append(direction)
    update_local = jnp.stack([jnp.sum(member * member) for member in directions])
    weight_norm = jnp.sqrt(totals[1:])
    update_norm = jnp.sqrt(sum_everywhere(update_local))
    trust = weight_norm / update_norm
    results = [activations, input_grad]
    for place, master in enumerate(masters):
        new_weight = master - RATE * trust[place] * directions[place]
        results += [new_moments[place], new_squares[place], new_weight]
    return (*results, grad_norm, jnp.stack([weight_norm, update_norm]))


def solution(mesh):
    by_token = P("docs", "seq", None)
    by_slot = P(None, ("docs", "seq"), None)
    by_row = P(("docs", "seq"), None)
    by_gain = P(None, ("docs", "seq"))
    return jax.shard_map(
        shards,
        mesh=mesh,
        in_specs=(by_token, by_token, by_slot, by_slot, by_token, P(), P())
        + (by_row,) * 15
        + (by_gain,) * 3,
        out_specs=(by_token, by_token) + (by_row,) * 15 + (by_gain,) * 3 + (P(), P()),
        check_vma=False,
    )
```

```python
import functools
import math

import jax
import jax.numpy as jnp
from jax import lax
from jax.experimental import pallas as pl
from jax.experimental.pallas import tpu as pltpu
from jax.sharding import PartitionSpec as P

HEADS = 8
HEAD_DIM = 128
STEP = 10
NORM_EPS = 1e-06
BETA_ONE = 0.9
BETA_TWO = 0.999
ADAM_EPS = 1e-06
DECAY = 0.01
RATE = 0.5
CLIP = 1.0
LANES = 128
LOG2E = math.log2(math.e)
SCALE = HEAD_DIM ** (-0.5)
BF = jnp.bfloat16
F32 = jnp.float32
VMEM_LIMIT = 56 * 1024 * 1024


def send(x, axis, bits):
    return lax.ppermute(x, axis, [(i, i ^ bits) for i in range(lax.axis_size(axis))])


def token(*done):
    total = jnp.zeros((), F32)
    for member in done:
        corner = lax.slice(member, (0,) * member.ndim, (1,) * member.ndim)
        total = total + corner.reshape(()).astype(F32) * 0
    return total


def after(x, *done):
    return x + token(*done).astype(x.dtype)


def pieces_of(block, axis):
    bit = lax.axis_size(axis) // 2
    pieces = {0: block}
    while bit:
        pieces.update({k | bit: send(piece, axis, bit) for k, piece in list(pieces.items())})
        bit //= 2
    return [pieces[k] for k in range(len(pieces))]


def pick(pieces, axis, device):
    away = lax.axis_index(axis) ^ device
    picked = pieces[0]
    for k in range(1, len(pieces)):
        picked = jnp.where(away == k, pieces[k], picked)
    return picked


def stack(pieces, axis, dim=0):
    return jnp.concatenate([pick(pieces, axis, j) for j in range(len(pieces))], axis=dim)


def swap(cut):
    me = lax.axis_index("seq")
    return [cut(me)] + [send(cut(me ^ k), "seq", k) for k in range(1, lax.axis_size("seq"))]


def halve(blocks, axis, stage, late=0.0, low=1):
    mine = (lax.axis_index(axis) >> stage) & 1
    pairs = blocks.reshape((-1, 2, low) + blocks.shape[1:])
    away = lax.dynamic_index_in_dim(pairs, 1 - mine, 1, False).astype(BF)
    kept = lax.dynamic_index_in_dim(pairs, mine, 1, False).astype(F32)
    total = (kept + late) + send(away, axis, 1 << stage).astype(F32)
    return total.reshape((-1,) + blocks.shape[1:])


def reduce_over(blocks, axis, stage=0, late=0.0):
    while blocks.shape[0] > 1:
        blocks = halve(blocks, axis, stage, late if blocks.shape[0] == 2 else 0.0)
        stage += 1
    return blocks[0]


def to_everyone(vectors):
    return lax.all_to_all(vectors, ("docs", "seq"), split_axis=0, concat_axis=0, tiled=True)


def dot(a, b):
    return lax.dot_general(a, b, (((1,), (0,)), ((), ())), preferred_element_type=F32)


def dot_nt(a, b):
    return lax.dot_general(a, b, (((1,), (1,)), ((), ())), preferred_element_type=F32)


def dot_tn(a, b):
    return lax.dot_general(a, b, (((0,), (0,)), ((), ())), preferred_element_type=F32)


def params():
    return pltpu.CompilerParams(vmem_limit_bytes=VMEM_LIMIT)


def rows_of(rows, cols):
    return pl.BlockSpec((rows, cols), lambda i: (i, 0))


def all_of(rows, cols):
    return pl.BlockSpec((rows, cols), lambda i: (0, 0))


def cheap():
    return pl.CostEstimate(flops=1, bytes_accessed=1, transcendentals=0)


def waits_for(count):
    return [pl.BlockSpec(memory_space=pl.ANY)] * count


def gate_kernel(*refs):
    pass


def gate(x, *waits):
    return pl.pallas_call(
        gate_kernel,
        in_specs=waits_for(1 + len(waits)),
        out_specs=pl.BlockSpec(memory_space=pl.ANY),
        out_shape=jax.ShapeDtypeStruct(x.shape, x.dtype),
        input_output_aliases={0: 0},
        cost_estimate=cheap(),
        name="gate",
    )(x, *waits)


def pack_memory_kernel(heads, partner, key, value, mate_key, mate_value, *outs):
    for device in range(outs[0].shape[1]):
        for h in range(heads):
            at = slice((device * heads + h) * HEAD_DIM, (device * heads + h + 1) * HEAD_DIM)
            outs[h][0, device, 0, :, :HEAD_DIM] = key[0, :, at]
            outs[h][0, device, 0, :, HEAD_DIM:] = value[0, :, at]
            outs[h][0, device, 1, :, :HEAD_DIM] = mate_key[0, :, at]
            outs[h][0, device, 1, :, HEAD_DIM:] = mate_value[0, :, at]


def pack_memory(partner, cache_keys, cache_values, heads, seq_count):
    docs, rows, width = cache_keys.shape
    own = pl.BlockSpec((1, rows, width), lambda i, p: (i, 0, 0))
    mate = pl.BlockSpec((1, rows, width), lambda i, p: (p[i], 0, 0))
    shape = (docs, seq_count, 2, rows, 2 * HEAD_DIM)
    return pl.pallas_call(
        functools.partial(pack_memory_kernel, heads),
        grid_spec=pltpu.PrefetchScalarGridSpec(
            num_scalar_prefetch=1,
            grid=(docs,),
            in_specs=[own, own, mate, mate],
            out_specs=[pl.BlockSpec((1,) + shape[1:], lambda i, p: (i, 0, 0, 0, 0))] * heads,
        ),
        out_shape=[jax.ShapeDtypeStruct(shape, BF)] * heads,
        compiler_params=params(),
        cost_estimate=cheap(),
        name="pack_memory",
    )(partner, cache_keys, cache_values, cache_keys, cache_values)


def pack_inner_kernel(raw, down, out):
    part = out.shape[1]
    at = 0
    for c in range(raw.shape[1] // part):
        out[at : at + raw.shape[0], :] = raw[:, c * part : (c + 1) * part]
        at += raw.shape[0]
    group = (out.shape[0] - at) // (down.shape[1] // part)
    rest = jnp.zeros((group - down.shape[0], part), F32)
    for c in range(down.shape[1] // part):
        rows = jnp.concatenate([down[:, c * part : (c + 1) * part], rest], axis=0)
        out[at : at + group, :] = rows.astype(BF)
        at += group


def pack_inner(raw, down, group, part):
    rows = raw.shape[0] * (raw.shape[1] // part) + group * (down.shape[1] // part)
    return pl.pallas_call(
        pack_inner_kernel,
        in_specs=[whole(raw), whole(down)],
        out_specs=whole(None),
        out_shape=jax.ShapeDtypeStruct((rows, part), BF),
        cost_estimate=cheap(),
        name="pack_inner",
    )(raw, down)


def rows_at(ref, place, rows):
    return ref.at[pl.ds(pl.multiple_of(place * rows, rows), rows)]


def whole_spec(member):
    return pl.BlockSpec(member.shape, lambda i, here, n=member.ndim: (0,) * n)


def tile_spec(rows, cols):
    return pl.BlockSpec((rows, cols), lambda i, here: (i, 0))


def fixed_spec(rows, cols):
    return pl.BlockSpec((rows, cols), lambda i, here: (0, 0))


def lay_kernel(here, *refs):
    pieces, out = refs[:-1], refs[-1]
    for k, piece in enumerate(pieces):

        @pl.when(here[0] ^ k == pl.program_id(0))
        def _(piece=piece):
            out[...] = piece[...]


def lay_out(here, pieces):
    rows, cols = pieces[0].shape
    return pl.pallas_call(
        lay_kernel,
        grid_spec=pltpu.PrefetchScalarGridSpec(
            num_scalar_prefetch=1,
            grid=(len(pieces),),
            in_specs=[whole_spec(piece) for piece in pieces],
            out_specs=tile_spec(rows, cols),
        ),
        out_shape=jax.ShapeDtypeStruct((len(pieces) * rows, cols), pieces[0].dtype),
        compiler_params=params(),
        cost_estimate=cheap(),
        name="lay_out",
    )(here, *pieces)


def find_words(near, memory, per_device):
    wide = near.astype(F32).T.astype(jnp.int32)
    count = wide.shape[0] // 2
    index = wide[:count] * 64 + wide[count:]
    slot = index & (memory - 1)
    source = slot >> (per_device.bit_length() - 1)
    place = source * (2 * per_device) + (slot & (per_device - 1))
    place = place + (index >> (memory.bit_length() - 1)) * per_device
    bit = jnp.left_shift(jnp.int32(1), place >> 7)
    lane = place & (LANES - 1)
    shape = (LANES, near.shape[0])
    rows = lax.broadcasted_iota(jnp.int32, shape, 0)
    found = jnp.zeros(shape, jnp.int32)
    for n in range(count):
        found = found | jnp.where(rows == lane[n : n + 1], bit[n : n + 1], 0)
    return found.T


def project_kernel(heads, seq, docs, memory, per_device, here, *refs):
    tokens, weights = refs[:seq], refs[seq : seq + docs]
    cosine, sine = refs[seq + docs : seq + docs + 2]
    x, normed, ql, qm, kl, vl, words, weight, gains, held = refs[-10:]
    width = x.shape[1]
    cols = 3 * heads * HEAD_DIM
    step = pl.program_id(0)

    @pl.when(step == 0)
    def _():
        for k in range(docs):
            rows = weights[k].shape[0]
            rows_at(weight, here[1] ^ k, rows)[...] = weights[k][:, :cols]
            rows_at(held, here[1] ^ k, rows)[...] = weights[k][:, cols : cols + LANES].astype(F32)
        for part in range(width // LANES):
            lanes = slice(part * LANES, (part + 1) * LANES)
            gains[:, lanes] = held[lanes, :].T[: gains.shape[0]]

    for k in range(seq):

        @pl.when(here[0] ^ k == step)
        def _(k=k):
            x[...] = tokens[k][:, :width]
            words[...] = find_words(tokens[k][:, width:], memory, per_device)

    values = x[...].astype(F32)
    scale = lax.rsqrt(jnp.mean(values * values, axis=-1, keepdims=True) + NORM_EPS)
    low = (values * scale * gains[0:1, :]).astype(BF)
    normed[...] = low
    out = dot(low, weight[...])
    cos, sin = cosine[...], sine[...]
    for h in range(heads):
        part = slice(h * HEAD_DIM, (h + 1) * HEAD_DIM)
        q, k, v = (
            out[:, (3 * h + j) * HEAD_DIM : (3 * h + j + 1) * HEAD_DIM] for j in range(3)
        )
        qm[:, part] = q.astype(BF)
        ql[:, part] = (q * cos + pltpu.roll(q, HEAD_DIM // 2, 1) * sin).astype(BF)
        kl[:, part] = (k * cos + pltpu.roll(k, HEAD_DIM // 2, 1) * sin).astype(BF)
        vl[:, part] = v.astype(BF)


def project(here, tokens, weights, cosine, sine, heads, memory, per_device, waits):
    rows = tokens[0].shape[0]
    width = tokens[0].shape[1] - LANES
    length = rows * len(tokens)
    cols = heads * HEAD_DIM
    low = jax.ShapeDtypeStruct((length, cols), BF)
    full = jax.ShapeDtypeStruct((length, width), BF)
    return pl.pallas_call(
        functools.partial(project_kernel, heads, len(tokens), len(weights), memory, per_device),
        grid_spec=pltpu.PrefetchScalarGridSpec(
            num_scalar_prefetch=1,
            grid=(len(tokens),),
            in_specs=[whole_spec(member) for member in (*tokens, *weights)]
            + [tile_spec(rows, HEAD_DIM)] * 2
            + waits_for(len(waits)),
            out_specs=[tile_spec(rows, width)] * 2
            + [tile_spec(rows, cols)] * 4
            + [tile_spec(rows, LANES), fixed_spec(width, 3 * cols), fixed_spec(8, width)],
            scratch_shapes=[pltpu.VMEM((width, LANES), F32)],
        ),
        out_shape=[
            full, full, low, low, low, low,
            jax.ShapeDtypeStruct((length, LANES), jnp.int32),
            jax.ShapeDtypeStruct((width, 3 * cols), BF),
            jax.ShapeDtypeStruct((8, width), F32),
        ],
        compiler_params=params(),
        cost_estimate=cheap(),
        name="project",
    )(here, *tokens, *weights, cosine, sine, *waits)


def feed_forward_kernel(heads, seq, docs, here, *refs):
    blended, packed, refs = refs[: seq * heads], refs[seq * heads :][:docs], refs[seq * heads + docs :]
    x, merge, gains, cotangent = refs[:4]
    blend, normed, active, grad_raw, back, middle_mine, raw, down = refs[4:]
    step = pl.program_id(0)
    hidden = down.shape[0]
    part = packed[0].shape[1]
    rows, group = raw.shape[0] // docs, hidden // docs

    @pl.when(step == 0)
    def _():
        for k in range(docs):
            at = 0
            for c in range(raw.shape[1] // part):
                cols = slice(c * part, (c + 1) * part)
                rows_at(raw, here[1] ^ k, rows)[:, cols] = packed[k][at : at + rows, :]
                at += rows
            for c in range(down.shape[1] // part):
                cols = slice(c * part, (c + 1) * part)
                rows_at(down, here[1] ^ k, group)[:, cols] = packed[k][at : at + group, :]
                at += group

    for k in range(seq):
        for h in range(heads):
            at = pl.multiple_of(((here[0] ^ k) * heads + h) * HEAD_DIM, HEAD_DIM)
            blend[:, pl.ds(at, HEAD_DIM)] = blended[k * heads + h][...]
    middle = x[...].astype(F32) + dot(blend[...], merge[...])

    @pl.when(step == here[0])
    def _():
        middle_mine[...] = middle

    scale = lax.rsqrt(jnp.mean(middle * middle, axis=-1, keepdims=True) + NORM_EPS)
    low = (middle * scale * gains[1:2, :]).astype(BF)
    normed[...] = low
    grad_active = dot_nt(cotangent[...], down[...])
    gate_up = dot(low, raw[...])
    gate, up = gate_up[:, :hidden], gate_up[:, hidden:]
    sigmoid = jax.nn.sigmoid(gate)
    silu = gate * sigmoid
    active[...] = (silu * up).astype(BF)
    grad_gate = grad_active * up * sigmoid * (1.0 + gate * (1.0 - sigmoid))
    grad_raw[:, :hidden] = grad_gate.astype(BF)
    grad_raw[:, hidden:] = (grad_active * silu).astype(BF)
    back[...] = dot_nt(grad_raw[...], raw[...]).astype(BF)


def feed_forward(here, blended, packed, x, merge, gains, cotangent, heads, hidden):
    length, width = x.shape
    seq, docs = len(blended) // heads, len(packed)
    rows = length // seq
    double = 2 * hidden
    return pl.pallas_call(
        functools.partial(feed_forward_kernel, heads, seq, docs),
        grid_spec=pltpu.PrefetchScalarGridSpec(
            num_scalar_prefetch=1,
            grid=(seq,),
            in_specs=[tile_spec(rows, HEAD_DIM)] * len(blended)
            + [whole_spec(member) for member in packed]
            + [tile_spec(rows, width), whole_spec(merge), whole_spec(gains)]
            + [tile_spec(rows, width)],
            out_specs=[
                tile_spec(rows, width),
                tile_spec(rows, width),
                tile_spec(rows, hidden),
                tile_spec(rows, double),
                tile_spec(rows, width),
                fixed_spec(rows, width),
                fixed_spec(width, double),
                fixed_spec(hidden, width),
            ],
        ),
        out_shape=[
            jax.ShapeDtypeStruct((length, width), BF),
            jax.ShapeDtypeStruct((length, width), BF),
            jax.ShapeDtypeStruct((length, hidden), BF),
            jax.ShapeDtypeStruct((length, double), BF),
            jax.ShapeDtypeStruct((length, width), BF),
            jax.ShapeDtypeStruct((rows, width), F32),
            jax.ShapeDtypeStruct((width, double), BF),
            jax.ShapeDtypeStruct((hidden, width), BF),
        ],
        compiler_params=params(),
        cost_estimate=cheap(),
        name="feed_forward",
    )(here, *blended, *packed, x, merge, gains, cotangent)


def lower_triangle(span):
    row = lax.broadcasted_iota(jnp.int32, (span, span), 0)
    return lax.broadcasted_iota(jnp.int32, (span, span), 1) <= row


def allowed(words, chunk, chunk_keys):
    tiles = chunk_keys // LANES
    parts = []
    for tile in range(tiles):
        bit = chunk * tiles + tile
        mask = (1 << bit) if bit < 31 else -(1 << 31)
        parts.append((words & jnp.int32(mask)) != 0)
    return parts


def select_tiles(parts, values, other):
    cut = [
        jnp.where(part, values[:, t * LANES : (t + 1) * LANES], other)
        for t, part in enumerate(parts)
    ]
    return jnp.concatenate(cut, axis=1)


def attend_local_kernel(heads, tiles, ql, kl, vl, out, high, total):
    span = ql.shape[0]
    factor = SCALE * LOG2E

    for tile in range(tiles):

        @pl.when(pl.program_id(0) == tile)
        def _(tile=tile):
            seen = lower_triangle(span)
            for h in range(heads):
                part = slice(h * HEAD_DIM, (h + 1) * HEAD_DIM)
                keys = (tile + 1) * span
                scores = dot_nt(ql[:, part], kl[:keys, part]) * factor
                last = jnp.where(seen, scores[:, tile * span :], -jnp.inf)
                scores = jnp.concatenate([scores[:, : tile * span], last], 1) if tile else last
                top = jnp.max(scores, axis=1, keepdims=True)
                expo = jnp.exp2(scores - top)
                high[:, part] = jnp.broadcast_to(top, (span, HEAD_DIM))
                weight = jnp.sum(expo, axis=1, keepdims=True)
                total[:, part] = jnp.broadcast_to(weight, (span, HEAD_DIM))
                out[:, part] = dot(expo.astype(BF), vl[:keys, part])


def attend_local(ql, kl, vl, heads):
    length, width = ql.shape
    span = min(256, length)
    wide = jax.ShapeDtypeStruct((length, width), F32)
    return pl.pallas_call(
        functools.partial(attend_local_kernel, heads, length // span),
        grid=(length // span,),
        in_specs=[rows_of(span, width), all_of(length, width), all_of(length, width)],
        out_specs=[rows_of(span, width)] * 3,
        out_shape=[wide] * 3,
        compiler_params=params(),
        cost_estimate=cheap(),
        name="attend_local",
    )(ql, kl, vl)


def attend_memory_kernel(chunk_keys, flag, qm, words, kv, local, high, total, *refs):
    out, low, lse = refs[-3:]
    factor = SCALE * LOG2E

    def finish(top, weight, sums):
        values = sums / weight
        out[...] = values
        low[...] = values.astype(BF)
        lse[...] = jnp.broadcast_to(top + jnp.log2(weight), lse.shape)

    @pl.when(flag[0] == 0)
    def _():
        finish(high[:, :1], total[:, :1], local[...])

    @pl.when(flag[0] > 0)
    def _():
        bits = words[...]
        query = qm[...]
        top, weight, sums = high[:, :1], total[:, :1], local[...]
        for chunk in range(kv.shape[0] // chunk_keys):
            here = slice(chunk * chunk_keys, (chunk + 1) * chunk_keys)
            scores = dot_nt(query, kv[here, :HEAD_DIM]) * factor
            scores = select_tiles(allowed(bits, chunk, chunk_keys), scores, -jnp.inf)
            new_top = jnp.maximum(top, jnp.max(scores, axis=1, keepdims=True))
            shrink = jnp.exp2(top - new_top)
            expo = jnp.exp2(scores - new_top)
            weight = weight * shrink + jnp.sum(expo, axis=1, keepdims=True)
            sums = sums * shrink + dot(expo.astype(BF), kv[here, HEAD_DIM:])
            top = new_top
        finish(top, weight, sums)


def head_rows(span, head):
    return pl.BlockSpec((span, HEAD_DIM), lambda i: (i, head))


def head_all(length, head):
    return pl.BlockSpec((length, HEAD_DIM), lambda i: (0, head))


def attend_memory(flag, qm, words, kv, local, high, total, head, waits):
    length = qm.shape[0]
    span = min(256, length)
    keys = kv.shape[0]
    return pl.pallas_call(
        functools.partial(attend_memory_kernel, min(1024, keys)),
        grid=(length // span,),
        in_specs=[
            pl.BlockSpec(memory_space=pltpu.SMEM),
            head_rows(span, head),
            rows_of(span, LANES),
            all_of(keys, 2 * HEAD_DIM),
            head_rows(span, head),
            head_rows(span, head),
            head_rows(span, head),
            *waits_for(len(waits)),
        ],
        out_specs=[rows_of(span, HEAD_DIM)] * 3,
        out_shape=[
            jax.ShapeDtypeStruct((length, HEAD_DIM), F32),
            jax.ShapeDtypeStruct((length, HEAD_DIM), BF),
            jax.ShapeDtypeStruct((length, HEAD_DIM), F32),
        ],
        compiler_params=params(),
        cost_estimate=cheap(),
        name="attend_memory",
    )(flag, qm, words, kv, local, high, total, *waits)


def attend_back_kernel(
    chunk_keys, tiles, flag, ql, qm, kl, vl, words, kv, att, go, lse, cosq, sinq, cosk, sink, *refs
):
    out, sum_k, sum_v, sum_q = refs[-4:]
    span = ql.shape[0]
    factor = SCALE * LOG2E
    step = pl.program_id(0)
    grad = go[...]
    delta = jnp.sum(grad.astype(F32) * att[...], axis=1, keepdims=True)
    level = lse[:, :1]

    @pl.when(step == 0)
    def _():
        sum_k[...] = jnp.zeros_like(sum_k)
        sum_v[...] = jnp.zeros_like(sum_v)

    for tile in range(tiles):

        @pl.when(step == tile)
        def _(tile=tile):
            keys = (tile + 1) * span
            query = ql[...]
            scores = dot_nt(query, kl[:keys]) * factor
            prob = jnp.exp2(scores - level)
            last = jnp.where(lower_triangle(span), prob[:, tile * span :], 0.0)
            prob = jnp.concatenate([prob[:, : tile * span], last], 1) if tile else last
            grad_prob = dot_nt(grad, vl[:keys])
            grad_scores = (prob * (grad_prob - delta)).astype(BF)
            sum_v[:keys] += dot_tn(prob.astype(BF), grad)
            sum_k[:keys] += dot_tn(grad_scores, query)
            back = dot(grad_scores, kl[:keys])
            sum_q[...] = back * cosq[...] - pltpu.roll(back, HEAD_DIM // 2, 1) * sinq[...]

    @pl.when(flag[0] > 0)
    def _():
        bits = words[...]
        query = qm[...]
        sums = sum_q[...]
        for chunk in range(kv.shape[0] // chunk_keys):
            here = slice(chunk * chunk_keys, (chunk + 1) * chunk_keys)
            key = kv[here, :HEAD_DIM]
            scores = dot_nt(query, key) * factor
            prob = jnp.exp2(scores - level)
            prob = select_tiles(allowed(bits, chunk, chunk_keys), prob, 0.0)
            grad_prob = dot_nt(grad, kv[here, HEAD_DIM:])
            grad_scores = (prob * (grad_prob - delta)).astype(BF)
            sums = sums + dot(grad_scores, key)
        sum_q[...] = sums

    here = pl.ds(pl.multiple_of(step * span, span), span)
    out[here, :HEAD_DIM] = (sum_q[...] * SCALE).astype(BF)

    @pl.when(step == tiles - 1)
    def _():
        back = sum_k[...] * SCALE
        back = back * cosk[...] - pltpu.roll(back, HEAD_DIM // 2, 1) * sink[...]
        out[:, HEAD_DIM : 2 * HEAD_DIM] = back.astype(BF)
        out[:, 2 * HEAD_DIM :] = sum_v[...].astype(BF)


def attend_back(flag, ql, qm, kl, vl, words, kv, att, go, lse, cosine, sine, head, waits):
    length = ql.shape[0]
    span = min(256, length)
    keys = kv.shape[0]
    return pl.pallas_call(
        functools.partial(attend_back_kernel, min(1024, keys), length // span),
        grid=(length // span,),
        in_specs=[
            pl.BlockSpec(memory_space=pltpu.SMEM),
            head_rows(span, head),
            head_rows(span, head),
            head_all(length, head),
            head_all(length, head),
            rows_of(span, LANES),
            all_of(keys, 2 * HEAD_DIM),
            rows_of(span, HEAD_DIM),
            head_rows(span, head),
            rows_of(span, HEAD_DIM),
            rows_of(span, HEAD_DIM),
            rows_of(span, HEAD_DIM),
            all_of(length, HEAD_DIM),
            all_of(length, HEAD_DIM),
            *waits_for(len(waits)),
        ],
        out_specs=all_of(length, 3 * HEAD_DIM),
        out_shape=jax.ShapeDtypeStruct((length, 3 * HEAD_DIM), BF),
        scratch_shapes=[
            pltpu.VMEM((length, HEAD_DIM), F32),
            pltpu.VMEM((length, HEAD_DIM), F32),
            pltpu.VMEM((span, HEAD_DIM), F32),
        ],
        compiler_params=params(),
        cost_estimate=cheap(),
        name="attend_back",
    )(flag, ql, qm, kl, vl, words, kv, att, go, lse, cosine, sine, cosine, sine, *waits)


def total_of(member):
    return jnp.sum(jnp.sum(member * member, axis=1, keepdims=True), axis=0, keepdims=True)


def lanes_of(values):
    lane = lax.broadcasted_iota(jnp.int32, (1, LANES), 1)
    row = jnp.zeros((1, LANES), F32)
    for place, value in enumerate(values):
        row = jnp.where(lane == place, value, row)
    return row


def row_of(column):
    shape = (column.shape[0], column.shape[0])
    same = lax.broadcasted_iota(jnp.int32, shape, 0) == lax.broadcasted_iota(jnp.int32, shape, 1)
    return jnp.sum(jnp.where(same, column, 0.0), axis=0, keepdims=True)


def grads_kernel(heads, docs, *refs):
    masters, by_head = refs[:6], refs[6]
    merge, raw, down = refs[7:10]
    g_heads, gate, up, g_gains, sums = refs[-5:]
    rows = g_heads.shape[0]
    width = g_heads.shape[1] // 3
    count = by_head.shape[1] // (3 * HEAD_DIM * heads)
    for device in range(count):
        for h in range(heads):
            for j in range(3):
                at = (3 * (device * heads + h) + j) * HEAD_DIM
                to = j * width + (device * heads + h) * HEAD_DIM
                part = by_head[:, at : at + HEAD_DIM].astype(F32)
                g_heads[:, to : to + HEAD_DIM] = part
    seq = raw.shape[0] // rows
    group, part = raw.shape[1] // (2 * docs), gate.shape[1] // (docs * seq)
    for device in range(seq):
        lines = slice(device * rows, (device + 1) * rows)
        for d in range(docs):
            to = (d * seq + device) * part
            for j, target in enumerate((gate, up)):
                at = (j * docs + d) * group
                target[:, to : to + part] = raw[lines, at : at + part].astype(F32)
    low = masters[0][...].astype(BF).astype(F32)
    gain_one = jnp.sum(g_heads[...] * low, axis=1, keepdims=True)
    gain_two = jnp.sum(
        gate[...] * masters[2][...].astype(BF).astype(F32)
        + up[...] * masters[3][...].astype(BF).astype(F32),
        axis=1,
        keepdims=True,
    )
    gain_low = masters[5][...].astype(BF).astype(F32)
    g_gains[0:1, :] = row_of(gain_one) / gain_low[0:1]
    g_gains[1:2, :] = row_of(gain_two) / gain_low[1:2]
    grad = [total_of(ref[...]) for ref in (g_heads, merge, gate, up, down, g_gains)]
    row = lanes_of([sum(grad)] + [total_of(ref[...]) for ref in masters])
    sums[...] = jnp.broadcast_to(row[None], sums.shape)


def whole(ref_or_array):
    return pl.BlockSpec(memory_space=pltpu.VMEM)


def grads(masters, by_head, merge, raw, down, devices, heads, docs, waits):
    inputs = [*masters, by_head, merge, raw, down]
    return pl.pallas_call(
        functools.partial(grads_kernel, heads, docs),
        in_specs=[whole(member) for member in inputs] + waits_for(len(waits)),
        out_specs=[whole(None)] * 5,
        out_shape=[
            jax.ShapeDtypeStruct(masters[0].shape, F32),
            jax.ShapeDtypeStruct(masters[2].shape, F32),
            jax.ShapeDtypeStruct(masters[3].shape, F32),
            jax.ShapeDtypeStruct(masters[5].shape, F32),
            jax.ShapeDtypeStruct((devices, 1, LANES), F32),
        ],
        compiler_params=params(),
        cost_estimate=cheap(),
        name="grads",
    )(*inputs, *waits)


def moments_kernel(*refs):
    totals, refs = refs[0], refs[1:]
    masters, old_moments, old_squares, gradients = (refs[6 * j : 6 * j + 6] for j in range(4))
    moments, squares, directions = (refs[6 * j - 19 : 6 * j - 13] for j in range(3))
    sums = refs[-1]
    total = jnp.sum(totals[...], axis=0)
    factor = CLIP / jnp.maximum(jnp.sqrt(total[:, 0:1]), CLIP)
    fix_one = 1.0 - BETA_ONE**STEP
    fix_two = 1.0 - BETA_TWO**STEP
    norms = []
    for place in range(6):
        clipped = factor * gradients[place][...]
        moment = BETA_ONE * old_moments[place][...] + (1.0 - BETA_ONE) * clipped
        square = BETA_TWO * old_squares[place][...] + (1.0 - BETA_TWO) * clipped * clipped
        direction = moment / fix_one / (jnp.sqrt(square / fix_two) + ADAM_EPS)
        if place < 5:
            direction = direction + DECAY * masters[place][...]
        moments[place][...] = moment
        squares[place][...] = square
        directions[place][...] = direction
        norms.append(total_of(direction))
    sums[...] = jnp.broadcast_to(lanes_of(norms)[None], sums.shape)


def step_moments(totals, masters, moments, squares, gradients, waits):
    inputs = [totals, *masters, *moments, *squares, *gradients]
    shapes = [jax.ShapeDtypeStruct(member.shape, F32) for member in masters]
    out = pl.pallas_call(
        moments_kernel,
        in_specs=[whole(member) for member in inputs] + waits_for(len(waits)),
        out_specs=[whole(None)] * 19,
        out_shape=shapes * 3 + [jax.ShapeDtypeStruct(totals.shape, F32)],
        compiler_params=params(),
        cost_estimate=cheap(),
        name="moments",
    )(*inputs, *waits)
    return out[:6], out[6:12], out[12:18], out[18]


def weights_kernel(*refs):
    totals, updates, refs = refs[0], refs[1], refs[2:]
    masters, directions, fresh = refs[:6], refs[6:12], refs[-8:-2]
    norms, clip = refs[-2:]
    old = jnp.sqrt(jnp.sum(totals[...], axis=0))
    new = jnp.sqrt(jnp.sum(updates[...], axis=0))
    for place in range(6):
        trust = old[:, place + 1 : place + 2] / new[:, place : place + 1]
        fresh[place][...] = masters[place][...] - RATE * trust * directions[place][...]
    norms[0:1, :] = pltpu.roll(old, LANES - 1, 1)
    norms[1:2, :] = new
    clip[...] = old


def step_weights(totals, updates, masters, directions, waits):
    inputs = [totals, updates, *masters, *directions]
    shapes = [jax.ShapeDtypeStruct(member.shape, F32) for member in masters]
    out = pl.pallas_call(
        weights_kernel,
        in_specs=[whole(member) for member in inputs] + waits_for(len(waits)),
        out_specs=[whole(None)] * 8,
        out_shape=shapes
        + [jax.ShapeDtypeStruct((2, LANES), F32), jax.ShapeDtypeStruct((1, LANES), F32)],
        compiler_params=params(),
        cost_estimate=cheap(),
        name="weights",
    )(*inputs, *waits)
    return out[:6], out[6][:, :6], out[7][0, 0]


def norm_rows(values):
    row_scale = lax.rsqrt(jnp.mean(values * values, axis=-1, keepdims=True) + NORM_EPS)
    return (values * row_scale, row_scale)


def norm_back(grad_normed, unit_rows, row_scale, gain_row):
    weighted = grad_normed * gain_row
    inner = jnp.mean(weighted * unit_rows, axis=-1, keepdims=True)
    return row_scale * (weighted - unit_rows * inner)


def rotation(length):
    half = HEAD_DIM // 2
    frequency = jnp.exp(-jnp.log(10000.0) * jnp.arange(half, dtype=F32) / half)
    grid = jnp.arange(length, dtype=F32)[:, None] * frequency[None, :]
    cos, sin = jnp.cos(grid), jnp.sin(grid)
    return jnp.concatenate([cos, cos], 1), jnp.concatenate([-sin, sin], 1)


def shards(
    tokens, cotangent, cache_keys, cache_values, neighbours, partner, has_memory,
    w_heads, moment_heads, square_heads, w_merge, moment_merge, square_merge,
    w_gate, moment_gate, square_gate, w_up, moment_up, square_up,
    w_down, moment_down, square_down, gains, moment_gains, square_gains,
):
    _, rows, width = tokens.shape
    seq_count = lax.axis_size("seq")
    docs_count = lax.axis_size("docs")
    devices = seq_count * docs_count
    seq_index = lax.axis_index("seq")
    doc_index = lax.axis_index("docs")
    here = jnp.stack([seq_index, doc_index]).astype(jnp.int32)
    length = rows * seq_count
    heads = HEADS // seq_count
    cols = heads * HEAD_DIM
    weight_rows = w_heads.shape[0]
    down_rows = w_down.shape[0]
    group = -(-down_rows // 16) * 16
    hidden = group * docs_count
    per_device = cache_keys.shape[1]
    masters = (w_heads, w_merge, w_gate, w_up, w_down, gains)
    moments = (moment_heads, moment_merge, moment_gate, moment_up, moment_down, moment_gains)
    squares = (square_heads, square_merge, square_gate, square_up, square_down, square_gains)

    low_heads = w_heads.astype(BF).reshape(weight_rows, 3, seq_count, heads, HEAD_DIM)
    low_heads = low_heads.transpose(2, 0, 3, 1, 4).reshape(seq_count, weight_rows, 3 * cols)
    gain_cols = jnp.pad(gains.astype(BF).T, ((0, 0), (0, LANES - 2)))
    first_block = stack(
        swap(
            lambda j: jnp.concatenate(
                [lax.dynamic_index_in_dim(low_heads, j, 0, False), gain_cols], axis=1
            )
        ),
        "seq",
    )
    merge_cols = width // seq_count
    low_merge = w_merge.astype(BF).reshape(weight_rows, seq_count, merge_cols).transpose(1, 0, 2)
    low_merge = low_merge.reshape(seq_count * weight_rows, merge_cols)
    first = pieces_of(jnp.concatenate([first_block, low_merge], axis=1), "docs")


    def columns(member):
        split = member.astype(BF).reshape(weight_rows, docs_count, seq_count, down_rows)
        split = jnp.pad(split.transpose(2, 0, 1, 3), ((0, 0), (0, 0), (0, 0), (0, group - down_rows)))
        return split.reshape(seq_count, weight_rows, hidden)

    low_raw = after(jnp.concatenate([columns(w_gate), columns(w_up)], axis=2), first_block)
    low_raw = stack(swap(lambda j: lax.dynamic_index_in_dim(low_raw, j, 0, False)), "seq")
    packed = pack_inner(low_raw, w_down, group, min(512, width))
    packed = pieces_of(packed, "docs")

    near = jnp.concatenate([neighbours[0] // 64, neighbours[0] % 64], axis=1).astype(BF)
    x_near = pieces_of(after(jnp.concatenate([tokens[0], near], axis=1), low_raw), "seq")
    flag = jnp.take(has_memory, doc_index[None])
    grad_low = pieces_of(after(cotangent[0], x_near[2 if seq_count > 2 else -1]), "seq")
    low_merge = stack([piece[:, 3 * cols + LANES :] for piece in first], "docs")
    low_merge = low_merge.reshape(docs_count, seq_count, weight_rows, merge_cols)
    low_merge = low_merge.transpose(0, 2, 1, 3).reshape(docs_count, weight_rows, width)
    low_merge = pieces_of(low_merge, "seq")
    merge_full = jnp.stack([pick(low_merge, "seq", j) for j in range(seq_count)], axis=1)
    merge_full = merge_full.reshape(width, width)

    waits = (*first[1:], *packed[1:5], *packed[6:7], *x_near[1:], *grad_low[1:], *low_merge[1:])
    grad_low = lay_out(here, grad_low)
    gated, memory = [], []
    for member in pack_memory(partner, cache_keys, cache_values, heads, seq_count):
        gated.append(gate(member.reshape(devices, 2, per_device, 2 * HEAD_DIM), *waits))
        member = lax.all_to_all(
            gated[-1], ("docs", "seq"), split_axis=0, concat_axis=0, tiled=True
        )
        memory.append(member.reshape(devices * 2 * per_device, 2 * HEAD_DIM))
        waits = (memory[0], *packed[5:])
    cosine, sine = rotation(length)
    (
        x_low, normed_one, query_local, query_memory, key_local, value_local, words, heads_here, gain_rows,
    ) = project(here, x_near, first, cosine, sine, heads, per_device * devices, per_device,
      gated[:1])
    local, high, total = attend_local(query_local, key_local, value_local, heads)


    attended, blended, lse = [], [], []
    for h in range(heads):
        result = attend_memory(
            flag, query_memory, words, memory[h], local, high, total, h, (grad_low, merge_full)
        )
        attended.append(result[0])
        blended.append(pieces_of(result[1], "seq"))
        lse.append(result[2])

    blended, normed_two, active, grad_raw, back, middle, _, down_here = feed_forward(
        here, [piece for pieces in zip(*blended) for piece in pieces], packed,
        x_low, merge_full, gain_rows, grad_low, heads, hidden,
    )
    grad_normed_two = halve(back.reshape(seq_count, rows, width), "seq", 0)
    bits = docs_count.bit_length() - 1
    g_gate, g_up = (
        dot_tn(normed_two, grad_raw[:, j * hidden : (j + 1) * hidden]).astype(BF) for j in range(2)
    )
    g_down = dot_tn(active, grad_low).astype(BF).reshape(docs_count, group, width)
    grad_normed_two = reduce_over(grad_normed_two, "seq", 1)
    unit_two, scale_two = norm_rows(middle)
    grad_middle = cotangent[0].astype(F32) + norm_back(
        grad_normed_two, unit_two, scale_two, gain_rows[1:2]
    )
    grad_branch = grad_middle.astype(BF)
    grad_mine = dot_nt(grad_branch, merge_full).astype(BF)
    grad_attended = stack(swap(lambda j: lax.dynamic_slice_in_dim(grad_mine, j * cols, cols, 1)), "seq")

    down_out = dot(active, down_here).astype(BF).reshape(seq_count, rows, width)
    down_out = halve(down_out, "seq", 0)
    waits = (g_gate, g_up, g_down, down_out)
    g_gate = g_gate.reshape(docs_count, width // docs_count, hidden)
    g_gate = halve(g_gate, "docs", 0, token(grad_attended))
    g_up = g_up.reshape(docs_count, width // docs_count, hidden)
    branches = pieces_of(gate(grad_branch, grad_attended), "seq")

    projected, by_head = [], []
    for h in range(heads):
        projected.append(
            attend_back(
                flag, query_local, query_memory, key_local, value_local, words,
                memory[h], attended[h], grad_attended, lse[h], cosine, sine, h, waits,
            )
        )
        g_heads = dot_tn(normed_one, projected[h]).astype(BF)
        by_head.append(g_heads.reshape(docs_count, width // docs_count, 3 * HEAD_DIM))
        if h == 0:
            halfway = token(projected[0])
            down_out = gate(down_out, projected[0])
            g_gate = halve(g_gate, "docs", 1, halfway)
            g_up = halve(g_up, "docs", 0, halfway)
            g_down = halve(g_down, "docs", 0, halfway)
            waits = (g_heads, g_gate, g_up, g_down, *branches[1:])
    last = token(projected[-1])
    down_out = reduce_over(down_out, "seq", 1, last)
    activations = (middle + down_out).astype(BF)[None]
    by_head = [halve(member, "docs", 0, last) for member in by_head]
    begun = token(by_head[-1])
    g_gate = halve(g_gate, "docs", 2, begun) if bits > 2 else g_gate
    g_gate = reduce_over(g_gate, "docs", 3)
    g_up = reduce_over(halve(g_up, "docs", 1, last), "docs", 2, begun)
    g_down = reduce_over(halve(g_down, "docs", 1, last), "docs", 2, begun)[:down_rows]
    g_raw = jnp.concatenate([g_gate, g_up], axis=1)
    g_merge = (dot_tn(blended, stack(branches, "seq")) + begun).astype(BF)
    g_merge = g_merge.reshape(docs_count, seq_count, weight_rows, width)
    g_merge = lax.dynamic_index_in_dim(g_merge, seq_index, 1, False)
    by_head = jnp.concatenate(by_head, axis=2)
    g_merge = reduce_over(g_merge, "docs")
    def own_rows(member):
        member = member.astype(BF).reshape(seq_count, weight_rows, member.shape[1])
        return swap(lambda j: lax.dynamic_index_in_dim(member, j, 0, False))

    g_raw = stack(own_rows(g_raw), "seq")
    by_head = stack(own_rows(reduce_over(by_head, "docs", 1)), "seq", 1)
    grad_projected = jnp.concatenate(projected, axis=1)
    grad_normed_one = (dot_nt(grad_projected, heads_here) + begun).astype(BF)
    grad_normed_one = halve(grad_normed_one.reshape(seq_count, rows, width), "seq", 0)
    waits = (grad_normed_one, activations)
    grad_normed_one = reduce_over(grad_normed_one, "seq", 1)
    unit_one, scale_one = norm_rows(tokens[0].astype(F32))
    input_grad = grad_middle + norm_back(grad_normed_one, unit_one, scale_one, gain_rows[0:1])
    input_grad = input_grad[None]

    g_heads, g_gate, g_up, g_gains, totals = grads(
        masters, by_head, g_merge, g_raw, g_down, devices, heads, docs_count, waits
    )
    gradients = (g_heads, g_merge, g_gate, g_up, g_down, g_gains)
    totals = to_everyone(totals)
    new_moments, new_squares, directions, updates = step_moments(
        totals, masters, moments, squares, gradients, ()
    )
    new_weights, layer_norms, clip_norm = step_weights(
        totals, to_everyone(updates), masters, directions, (input_grad,)
    )
    results = [activations, input_grad]
    for place in range(6):
        results += [new_moments[place], new_squares[place], new_weights[place]]
    return (*results, clip_norm, layer_norms)


def solution(mesh):
    by_token = P("docs", "seq", None)
    by_slot = P(None, ("docs", "seq"), None)
    by_row = P(("docs", "seq"), None)
    by_gain = P(None, ("docs", "seq"))
    return jax.shard_map(
        shards,
        mesh=mesh,
        in_specs=(by_token, by_token, by_slot, by_slot, by_token, P(), P())
        + (by_row,) * 15
        + (by_gain,) * 3,
        out_specs=(by_token, by_token) + (by_row,) * 15 + (by_gain,) * 3 + (P(), P()),
        check_vma=False,
    )
```

```python
import functools
import math

import jax
import jax.numpy as jnp
from jax import lax
from jax.experimental import pallas as pl
from jax.experimental.pallas import tpu as pltpu
from jax.sharding import PartitionSpec as P

HEADS = 8
HEAD_DIM = 128
STEP = 10
NORM_EPS = 1e-06
BETA_ONE = 0.9
BETA_TWO = 0.999
ADAM_EPS = 1e-06
DECAY = 0.01
RATE = 0.5
CLIP = 1.0
LANES = 128
LOG2E = math.log2(math.e)
SCALE = HEAD_DIM ** (-0.5)
BF = jnp.bfloat16
F32 = jnp.float32


def send(x, axis, bits):
    return lax.ppermute(x, axis, [(i, i ^ bits) for i in range(lax.axis_size(axis))])


def token(*done):
    total = jnp.zeros((), F32)
    for member in done:
        corner = lax.slice(member, (0,) * member.ndim, (1,) * member.ndim)
        total = total + corner.reshape(()).astype(F32) * 0
    return total


def after(x, *done):
    return x + token(*done).astype(x.dtype)


def pieces_of(block, axis):
    bit = lax.axis_size(axis) // 2
    pieces = {0: block}
    while bit:
        pieces.update({k | bit: send(piece, axis, bit) for k, piece in list(pieces.items())})
        bit //= 2
    return [pieces[k] for k in range(len(pieces))]


def pick(pieces, axis, device):
    away = lax.axis_index(axis) ^ device
    picked = pieces[0]
    for k in range(1, len(pieces)):
        picked = jnp.where(away == k, pieces[k], picked)
    return picked


def stack(pieces, axis, dim=0):
    return jnp.concatenate([pick(pieces, axis, j) for j in range(len(pieces))], axis=dim)


def swap(cut):
    me = lax.axis_index("seq")
    return [cut(me)] + [send(cut(me ^ k), "seq", k) for k in range(1, lax.axis_size("seq"))]


def halve(blocks, axis, stage, late=0.0, low=1):
    mine = (lax.axis_index(axis) >> stage) & 1
    pairs = blocks.reshape((-1, 2, low) + blocks.shape[1:])
    away = lax.dynamic_index_in_dim(pairs, 1 - mine, 1, False).astype(BF)
    kept = lax.dynamic_index_in_dim(pairs, mine, 1, False).astype(F32)
    total = (kept + late) + send(away, axis, 1 << stage).astype(F32)
    return total.reshape((-1,) + blocks.shape[1:])


def reduce_over(blocks, axis, stage=0, late=0.0):
    while blocks.shape[0] > 1:
        blocks = halve(blocks, axis, stage, late if blocks.shape[0] == 2 else 0.0)
        stage += 1
    return blocks[0]


def to_everyone(vectors):
    return lax.all_to_all(vectors, ("docs", "seq"), split_axis=0, concat_axis=0, tiled=True)


def dot(a, b):
    return lax.dot_general(a, b, (((1,), (0,)), ((), ())), preferred_element_type=F32)


def dot_nt(a, b):
    return lax.dot_general(a, b, (((1,), (1,)), ((), ())), preferred_element_type=F32)


def dot_tn(a, b):
    return lax.dot_general(a, b, (((0,), (0,)), ((), ())), preferred_element_type=F32)


def params(mebibytes=56):
    return pltpu.CompilerParams(vmem_limit_bytes=mebibytes * 1024 * 1024)


def rows_of(rows, cols):
    return pl.BlockSpec((rows, cols), lambda i: (i, 0))


def all_of(rows, cols):
    return pl.BlockSpec((rows, cols), lambda i: (0, 0))


def cheap():
    return pl.CostEstimate(flops=1, bytes_accessed=1, transcendentals=0)


def waits_for(count):
    return [pl.BlockSpec(memory_space=pl.ANY)] * count


def gate_kernel(*refs):
    pass


def gate(x, *waits):
    return pl.pallas_call(
        gate_kernel,
        in_specs=waits_for(1 + len(waits)),
        out_specs=pl.BlockSpec(memory_space=pl.ANY),
        out_shape=jax.ShapeDtypeStruct(x.shape, x.dtype),
        input_output_aliases={0: 0},
        cost_estimate=cheap(),
        name="gate",
    )(x, *waits)


def pack_memory_kernel(heads, partner, key, value, mate_key, mate_value, *outs):
    for device in range(outs[0].shape[1]):
        for h in range(heads):
            at = slice((device * heads + h) * HEAD_DIM, (device * heads + h + 1) * HEAD_DIM)
            outs[h][0, device, 0, :, :HEAD_DIM] = key[0, :, at]
            outs[h][0, device, 0, :, HEAD_DIM:] = value[0, :, at]
            outs[h][0, device, 1, :, :HEAD_DIM] = mate_key[0, :, at]
            outs[h][0, device, 1, :, HEAD_DIM:] = mate_value[0, :, at]


def pack_memory(partner, cache_keys, cache_values, heads, seq_count):
    docs, rows, width = cache_keys.shape
    own = pl.BlockSpec((1, rows, width), lambda i, p: (i, 0, 0))
    mate = pl.BlockSpec((1, rows, width), lambda i, p: (p[i], 0, 0))
    shape = (docs, seq_count, 2, rows, 2 * HEAD_DIM)
    return pl.pallas_call(
        functools.partial(pack_memory_kernel, heads),
        grid_spec=pltpu.PrefetchScalarGridSpec(
            num_scalar_prefetch=1,
            grid=(docs,),
            in_specs=[own, own, mate, mate],
            out_specs=[pl.BlockSpec((1,) + shape[1:], lambda i, p: (i, 0, 0, 0, 0))] * heads,
        ),
        out_shape=[jax.ShapeDtypeStruct(shape, BF)] * heads,
        compiler_params=params(),
        cost_estimate=cheap(),
        name="pack_memory",
    )(partner, cache_keys, cache_values, cache_keys, cache_values)


def pack_inner_kernel(raw, down, out):
    part = out.shape[1]
    at = 0
    for c in range(raw.shape[1] // part):
        out[at : at + raw.shape[0], :] = raw[:, c * part : (c + 1) * part]
        at += raw.shape[0]
    group = (out.shape[0] - at) // (down.shape[1] // part)
    rest = jnp.zeros((group - down.shape[0], part), F32)
    for c in range(down.shape[1] // part):
        rows = jnp.concatenate([down[:, c * part : (c + 1) * part], rest], axis=0)
        out[at : at + group, :] = rows.astype(BF)
        at += group


def pack_inner(raw, down, group, part):
    rows = raw.shape[0] * (raw.shape[1] // part) + group * (down.shape[1] // part)
    return pl.pallas_call(
        pack_inner_kernel,
        in_specs=[whole(raw), whole(down)],
        out_specs=whole(None),
        out_shape=jax.ShapeDtypeStruct((rows, part), BF),
        cost_estimate=cheap(),
        name="pack_inner",
    )(raw, down)


def rows_at(ref, place, rows):
    return ref.at[pl.ds(pl.multiple_of(place * rows, rows), rows)]


def whole_spec(member):
    return pl.BlockSpec(member.shape, lambda i, here, n=member.ndim: (0,) * n)


def tile_spec(rows, cols):
    return pl.BlockSpec((rows, cols), lambda i, here: (i, 0))


def fixed_spec(rows, cols):
    return pl.BlockSpec((rows, cols), lambda i, here: (0, 0))


def lay_kernel(here, *refs):
    pieces, out = refs[:-1], refs[-1]
    for k, piece in enumerate(pieces):

        @pl.when(here[0] ^ k == pl.program_id(0))
        def _(piece=piece):
            out[...] = piece[...]


def lay_out(here, pieces):
    rows, cols = pieces[0].shape
    return pl.pallas_call(
        lay_kernel,
        grid_spec=pltpu.PrefetchScalarGridSpec(
            num_scalar_prefetch=1,
            grid=(len(pieces),),
            in_specs=[whole_spec(piece) for piece in pieces],
            out_specs=tile_spec(rows, cols),
        ),
        out_shape=jax.ShapeDtypeStruct((len(pieces) * rows, cols), pieces[0].dtype),
        compiler_params=params(),
        cost_estimate=cheap(),
        name="lay_out",
    )(here, *pieces)


def find_words(near, memory, per_device):
    wide = near.astype(F32).T.astype(jnp.int32)
    count = wide.shape[0] // 2
    index = wide[:count] * 64 + wide[count:]
    slot = index & (memory - 1)
    source = slot >> (per_device.bit_length() - 1)
    place = source * (2 * per_device) + (slot & (per_device - 1))
    place = place + (index >> (memory.bit_length() - 1)) * per_device
    bit = jnp.left_shift(jnp.int32(1), place >> 7)
    lane = place & (LANES - 1)
    shape = (LANES, near.shape[0])
    rows = lax.broadcasted_iota(jnp.int32, shape, 0)
    found = jnp.zeros(shape, jnp.int32)
    for n in range(count):
        found = found | jnp.where(rows == lane[n : n + 1], bit[n : n + 1], 0)
    return found.T


def project_kernel(heads, seq, docs, memory, per_device, here, *refs):
    tokens, weights = refs[:seq], refs[seq : seq + docs]
    cosine, sine = refs[seq + docs : seq + docs + 2]
    x, normed, ql, qm, kl, vl, words, weight, gains, held = refs[-10:]
    width = x.shape[1]
    cols = 3 * heads * HEAD_DIM
    step = pl.program_id(0)

    @pl.when(step == 0)
    def _():
        for k in range(docs):
            rows = weights[k].shape[0]
            rows_at(weight, here[1] ^ k, rows)[...] = weights[k][:, :cols]
            rows_at(held, here[1] ^ k, rows)[...] = weights[k][:, cols : cols + LANES].astype(F32)
        for part in range(width // LANES):
            lanes = slice(part * LANES, (part + 1) * LANES)
            gains[:, lanes] = held[lanes, :].T[: gains.shape[0]]

    for k in range(seq):

        @pl.when(here[0] ^ k == step)
        def _(k=k):
            x[...] = tokens[k][:, :width]
            words[...] = find_words(tokens[k][:, width:], memory, per_device)

    values = x[...].astype(F32)
    scale = lax.rsqrt(jnp.mean(values * values, axis=-1, keepdims=True) + NORM_EPS)
    low = (values * scale * gains[0:1, :]).astype(BF)
    normed[...] = low
    out = dot(low, weight[...])
    cos, sin = cosine[...], sine[...]
    for h in range(heads):
        part = slice(h * HEAD_DIM, (h + 1) * HEAD_DIM)
        q, k, v = (
            out[:, (3 * h + j) * HEAD_DIM : (3 * h + j + 1) * HEAD_DIM] for j in range(3)
        )
        qm[:, part] = q.astype(BF)
        ql[:, part] = (q * cos + pltpu.roll(q, HEAD_DIM // 2, 1) * sin).astype(BF)
        kl[:, part] = (k * cos + pltpu.roll(k, HEAD_DIM // 2, 1) * sin).astype(BF)
        vl[:, part] = v.astype(BF)


def project(here, tokens, weights, cosine, sine, heads, memory, per_device, waits):
    rows = tokens[0].shape[0]
    width = tokens[0].shape[1] - LANES
    length = rows * len(tokens)
    cols = heads * HEAD_DIM
    low = jax.ShapeDtypeStruct((length, cols), BF)
    full = jax.ShapeDtypeStruct((length, width), BF)
    return pl.pallas_call(
        functools.partial(project_kernel, heads, len(tokens), len(weights), memory, per_device),
        grid_spec=pltpu.PrefetchScalarGridSpec(
            num_scalar_prefetch=1,
            grid=(len(tokens),),
            in_specs=[whole_spec(member) for member in (*tokens, *weights)]
            + [tile_spec(rows, HEAD_DIM)] * 2
            + waits_for(len(waits)),
            out_specs=[tile_spec(rows, width)] * 2
            + [tile_spec(rows, cols)] * 4
            + [tile_spec(rows, LANES), fixed_spec(width, 3 * cols), fixed_spec(8, width)],
            scratch_shapes=[pltpu.VMEM((width, LANES), F32)],
        ),
        out_shape=[
            full, full, low, low, low, low,
            jax.ShapeDtypeStruct((length, LANES), jnp.int32),
            jax.ShapeDtypeStruct((width, 3 * cols), BF),
            jax.ShapeDtypeStruct((8, width), F32),
        ],
        compiler_params=params(),
        cost_estimate=cheap(),
        name="project",
    )(here, *tokens, *weights, cosine, sine, *waits)


def feed_forward_kernel(heads, seq, docs, here, *refs):
    blended, packed, refs = refs[: seq * heads], refs[seq * heads :][:docs], refs[seq * heads + docs :]
    x, merge, gains, cotangent = refs[:4]
    blend, normed, active, grad_raw, back, middle_mine, raw, down = refs[4:]
    step = pl.program_id(0)
    hidden = down.shape[0]
    part = packed[0].shape[1]
    rows, group = raw.shape[0] // docs, hidden // docs

    @pl.when(step == 0)
    def _():
        for k in range(docs):
            at = 0
            for c in range(raw.shape[1] // part):
                cols = slice(c * part, (c + 1) * part)
                rows_at(raw, here[1] ^ k, rows)[:, cols] = packed[k][at : at + rows, :]
                at += rows
            for c in range(down.shape[1] // part):
                cols = slice(c * part, (c + 1) * part)
                rows_at(down, here[1] ^ k, group)[:, cols] = packed[k][at : at + group, :]
                at += group

    for k in range(seq):
        for h in range(heads):
            at = pl.multiple_of(((here[0] ^ k) * heads + h) * HEAD_DIM, HEAD_DIM)
            blend[:, pl.ds(at, HEAD_DIM)] = blended[k * heads + h][...]
    middle = x[...].astype(F32) + dot(blend[...], merge[...])

    @pl.when(step == here[0])
    def _():
        middle_mine[...] = middle

    scale = lax.rsqrt(jnp.mean(middle * middle, axis=-1, keepdims=True) + NORM_EPS)
    low = (middle * scale * gains[1:2, :]).astype(BF)
    normed[...] = low
    grad_active = dot_nt(cotangent[...], down[...])
    gate_up = dot(low, raw[...])
    gate, up = gate_up[:, :hidden], gate_up[:, hidden:]
    sigmoid = jax.nn.sigmoid(gate)
    silu = gate * sigmoid
    active[...] = (silu * up).astype(BF)
    grad_gate = grad_active * up * sigmoid * (1.0 + gate * (1.0 - sigmoid))
    grad_raw[:, :hidden] = grad_gate.astype(BF)
    grad_raw[:, hidden:] = (grad_active * silu).astype(BF)
    back[...] = dot_nt(grad_raw[...], raw[...]).astype(BF)


def feed_forward(here, blended, packed, x, merge, gains, cotangent, heads, hidden):
    length, width = x.shape
    seq, docs = len(blended) // heads, len(packed)
    rows = length // seq
    double = 2 * hidden
    return pl.pallas_call(
        functools.partial(feed_forward_kernel, heads, seq, docs),
        grid_spec=pltpu.PrefetchScalarGridSpec(
            num_scalar_prefetch=1,
            grid=(seq,),
            in_specs=[tile_spec(rows, HEAD_DIM)] * len(blended)
            + [whole_spec(member) for member in packed]
            + [tile_spec(rows, width), whole_spec(merge), whole_spec(gains)]
            + [tile_spec(rows, width)],
            out_specs=[
                tile_spec(rows, width),
                tile_spec(rows, width),
                tile_spec(rows, hidden),
                tile_spec(rows, double),
                tile_spec(rows, width),
                fixed_spec(rows, width),
                fixed_spec(width, double),
                fixed_spec(hidden, width),
            ],
        ),
        out_shape=[
            jax.ShapeDtypeStruct((length, width), BF),
            jax.ShapeDtypeStruct((length, width), BF),
            jax.ShapeDtypeStruct((length, hidden), BF),
            jax.ShapeDtypeStruct((length, double), BF),
            jax.ShapeDtypeStruct((length, width), BF),
            jax.ShapeDtypeStruct((rows, width), F32),
            jax.ShapeDtypeStruct((width, double), BF),
            jax.ShapeDtypeStruct((hidden, width), BF),
        ],
        compiler_params=params(),
        cost_estimate=cheap(),
        name="feed_forward",
    )(here, *blended, *packed, x, merge, gains, cotangent)


def lower_triangle(span):
    row = lax.broadcasted_iota(jnp.int32, (span, span), 0)
    return lax.broadcasted_iota(jnp.int32, (span, span), 1) <= row


def allowed(words, chunk, chunk_keys):
    tiles = chunk_keys // LANES
    parts = []
    for tile in range(tiles):
        bit = chunk * tiles + tile
        mask = (1 << bit) if bit < 31 else -(1 << 31)
        parts.append((words & jnp.int32(mask)) != 0)
    return parts


def select_tiles(parts, values, other):
    cut = [
        jnp.where(part, values[:, t * LANES : (t + 1) * LANES], other)
        for t, part in enumerate(parts)
    ]
    return jnp.concatenate(cut, axis=1)


def attend_local_kernel(heads, tiles, ql, kl, vl, out, high, total):
    span = ql.shape[0]
    factor = SCALE * LOG2E

    for tile in range(tiles):

        @pl.when(pl.program_id(0) == tile)
        def _(tile=tile):
            seen = lower_triangle(span)
            for h in range(heads):
                part = slice(h * HEAD_DIM, (h + 1) * HEAD_DIM)
                keys = (tile + 1) * span
                scores = dot_nt(ql[:, part], kl[:keys, part]) * factor
                last = jnp.where(seen, scores[:, tile * span :], -jnp.inf)
                scores = jnp.concatenate([scores[:, : tile * span], last], 1) if tile else last
                top = jnp.max(scores, axis=1, keepdims=True)
                expo = jnp.exp2(scores - top)
                high[:, part] = jnp.broadcast_to(top, (span, HEAD_DIM))
                weight = jnp.sum(expo, axis=1, keepdims=True)
                total[:, part] = jnp.broadcast_to(weight, (span, HEAD_DIM))
                out[:, part] = dot(expo.astype(BF), vl[:keys, part])


def attend_local(ql, kl, vl, heads):
    length, width = ql.shape
    span = min(512, length)
    wide = jax.ShapeDtypeStruct((length, width), F32)
    return pl.pallas_call(
        functools.partial(attend_local_kernel, heads, length // span),
        grid=(length // span,),
        in_specs=[rows_of(span, width), all_of(length, width), all_of(length, width)],
        out_specs=[rows_of(span, width)] * 3,
        out_shape=[wide] * 3,
        compiler_params=params(),
        cost_estimate=cheap(),
        name="attend_local",
    )(ql, kl, vl)


def attend_memory_kernel(chunk_keys, flag, qm, words, kv, local, high, total, *refs):
    out, low, lse = refs[-3:]
    factor = SCALE * LOG2E

    def finish(top, weight, sums):
        values = sums / weight
        out[...] = values
        low[...] = values.astype(BF)
        lse[...] = jnp.broadcast_to(top + jnp.log2(weight), lse.shape)

    @pl.when(flag[0] == 0)
    def _():
        finish(high[:, :1], total[:, :1], local[...])

    @pl.when(flag[0] > 0)
    def _():
        bits = words[...]
        query = qm[...]
        top, weight, sums = high[:, :1], total[:, :1], local[...]
        for chunk in range(kv.shape[0] // chunk_keys):
            here = slice(chunk * chunk_keys, (chunk + 1) * chunk_keys)
            scores = dot_nt(query, kv[here, :HEAD_DIM]) * factor
            scores = select_tiles(allowed(bits, chunk, chunk_keys), scores, -jnp.inf)
            new_top = jnp.maximum(top, jnp.max(scores, axis=1, keepdims=True))
            shrink = jnp.exp2(top - new_top)
            expo = jnp.exp2(scores - new_top)
            weight = weight * shrink + jnp.sum(expo, axis=1, keepdims=True)
            sums = sums * shrink + dot(expo.astype(BF), kv[here, HEAD_DIM:])
            top = new_top
        finish(top, weight, sums)


def head_rows(span, head):
    return pl.BlockSpec((span, HEAD_DIM), lambda i: (i, head))


def head_all(length, head):
    return pl.BlockSpec((length, HEAD_DIM), lambda i: (0, head))


def attend_memory(flag, qm, words, kv, local, high, total, head, waits):
    length = qm.shape[0]
    span = min(512, length)
    keys = kv.shape[0]
    return pl.pallas_call(
        functools.partial(attend_memory_kernel, min(4096, keys)),
        grid=(length // span,),
        in_specs=[
            pl.BlockSpec(memory_space=pltpu.SMEM),
            head_rows(span, head),
            rows_of(span, LANES),
            all_of(keys, 2 * HEAD_DIM),
            head_rows(span, head),
            head_rows(span, head),
            head_rows(span, head),
            *waits_for(len(waits)),
        ],
        out_specs=[rows_of(span, HEAD_DIM)] * 3,
        out_shape=[
            jax.ShapeDtypeStruct((length, HEAD_DIM), F32),
            jax.ShapeDtypeStruct((length, HEAD_DIM), BF),
            jax.ShapeDtypeStruct((length, HEAD_DIM), F32),
        ],
        compiler_params=params(),
        cost_estimate=cheap(),
        name="attend_memory",
    )(flag, qm, words, kv, local, high, total, *waits)


def attend_back_kernel(
    chunk_keys, tiles, flag, ql, qm, kl, vl, words, kv, att, go, lse, cosq, sinq, cosk, sink, *refs
):
    out, sum_k, sum_v, sum_q = refs[-4:]
    span = ql.shape[0]
    factor = SCALE * LOG2E
    step = pl.program_id(0)
    grad = go[...]
    delta = jnp.sum(grad.astype(F32) * att[...], axis=1, keepdims=True)
    level = lse[:, :1]

    @pl.when(step == 0)
    def _():
        sum_k[...] = jnp.zeros_like(sum_k)
        sum_v[...] = jnp.zeros_like(sum_v)

    for tile in range(tiles):

        @pl.when(step == tile)
        def _(tile=tile):
            keys = (tile + 1) * span
            query = ql[...]
            scores = dot_nt(query, kl[:keys]) * factor
            prob = jnp.exp2(scores - level)
            last = jnp.where(lower_triangle(span), prob[:, tile * span :], 0.0)
            prob = jnp.concatenate([prob[:, : tile * span], last], 1) if tile else last
            grad_prob = dot_nt(grad, vl[:keys])
            grad_scores = (prob * (grad_prob - delta)).astype(BF)
            sum_v[:keys] += dot_tn(prob.astype(BF), grad)
            sum_k[:keys] += dot_tn(grad_scores, query)
            back = dot(grad_scores, kl[:keys])
            sum_q[...] = back * cosq[...] - pltpu.roll(back, HEAD_DIM // 2, 1) * sinq[...]

    @pl.when(flag[0] > 0)
    def _():
        bits = words[...]
        query = qm[...]
        sums = sum_q[...]
        for chunk in range(kv.shape[0] // chunk_keys):
            here = slice(chunk * chunk_keys, (chunk + 1) * chunk_keys)
            key = kv[here, :HEAD_DIM]
            scores = dot_nt(query, key) * factor
            prob = jnp.exp2(scores - level)
            prob = select_tiles(allowed(bits, chunk, chunk_keys), prob, 0.0)
            grad_prob = dot_nt(grad, kv[here, HEAD_DIM:])
            grad_scores = (prob * (grad_prob - delta)).astype(BF)
            sums = sums + dot(grad_scores, key)
        sum_q[...] = sums

    here = pl.ds(pl.multiple_of(step * span, span), span)
    out[here, :HEAD_DIM] = (sum_q[...] * SCALE).astype(BF)

    @pl.when(step == tiles - 1)
    def _():
        back = sum_k[...] * SCALE
        back = back * cosk[...] - pltpu.roll(back, HEAD_DIM // 2, 1) * sink[...]
        out[:, HEAD_DIM : 2 * HEAD_DIM] = back.astype(BF)
        out[:, 2 * HEAD_DIM :] = sum_v[...].astype(BF)


def attend_back(flag, ql, qm, kl, vl, words, kv, att, go, lse, cosine, sine, head, waits):
    length, width = ql.shape
    span = min(512, length)
    keys = kv.shape[0]
    return pl.pallas_call(
        functools.partial(attend_back_kernel, min(512, keys), length // span),
        grid=(length // span,),
        in_specs=[
            pl.BlockSpec(memory_space=pltpu.SMEM),
            head_rows(span, head),
            head_rows(span, head),
            head_all(length, head),
            head_all(length, head),
            rows_of(span, LANES),
            all_of(keys, 2 * HEAD_DIM),
            rows_of(span, HEAD_DIM),
            head_rows(span, head),
            rows_of(span, HEAD_DIM),
            rows_of(span, HEAD_DIM),
            rows_of(span, HEAD_DIM),
            all_of(length, HEAD_DIM),
            all_of(length, HEAD_DIM),
            *waits_for(len(waits)),
        ],
        out_specs=all_of(length, 3 * HEAD_DIM),
        out_shape=jax.ShapeDtypeStruct((length, 3 * HEAD_DIM), BF),
        scratch_shapes=[
            pltpu.VMEM((length, HEAD_DIM), F32),
            pltpu.VMEM((length, HEAD_DIM), F32),
            pltpu.VMEM((span, HEAD_DIM), F32),
        ],
        compiler_params=params(),
        cost_estimate=pl.CostEstimate(
            flops=16 * 10**9, bytes_accessed=8 * length * width, transcendentals=length * keys
        ),
        name="attend_back",
    )(flag, ql, qm, kl, vl, words, kv, att, go, lse, cosine, sine, cosine, sine, *waits)


def total_of(member):
    return jnp.sum(jnp.sum(member * member, axis=1, keepdims=True), axis=0, keepdims=True)


def lanes_of(values):
    lane = lax.broadcasted_iota(jnp.int32, (1, LANES), 1)
    row = jnp.zeros((1, LANES), F32)
    for place, value in enumerate(values):
        row = jnp.where(lane == place, value, row)
    return row


def row_of(column):
    shape = (column.shape[0], column.shape[0])
    same = lax.broadcasted_iota(jnp.int32, shape, 0) == lax.broadcasted_iota(jnp.int32, shape, 1)
    return jnp.sum(jnp.where(same, column, 0.0), axis=0, keepdims=True)


def grads_kernel(heads, docs, *refs):
    masters = refs[:6]
    swapped, merge, down, g_heads, gate, up, g_gains, sums = refs[6:]
    rows = g_heads.shape[0]
    width = g_heads.shape[1] // 3
    seq = swapped.shape[0] // rows
    cols = 3 * HEAD_DIM * heads
    group, part = (swapped.shape[1] - cols) // (2 * docs), gate.shape[1] // (docs * seq)
    for device in range(seq):
        lines = slice(device * rows, (device + 1) * rows)
        for h in range(heads):
            for j in range(3):
                at = swapped.shape[1] - cols + (3 * (heads - 1 - h) + j) * HEAD_DIM
                to = j * width + (device * heads + h) * HEAD_DIM
                g_heads[:, to : to + HEAD_DIM] = swapped[lines, at : at + HEAD_DIM].astype(F32)
        for d in range(docs):
            to = (d * seq + device) * part
            for j, target in enumerate((gate, up)):
                at = (j * docs + d) * group
                target[:, to : to + part] = swapped[lines, at : at + part].astype(F32)
    low = masters[0][...].astype(BF).astype(F32)
    gain_one = jnp.sum(g_heads[...] * low, axis=1, keepdims=True)
    gain_two = jnp.sum(
        gate[...] * masters[2][...].astype(BF).astype(F32)
        + up[...] * masters[3][...].astype(BF).astype(F32),
        axis=1,
        keepdims=True,
    )
    gain_low = masters[5][...].astype(BF).astype(F32)
    g_gains[0:1, :] = row_of(gain_one) / gain_low[0:1]
    g_gains[1:2, :] = row_of(gain_two) / gain_low[1:2]
    grad = [total_of(ref[...]) for ref in (g_heads, merge, gate, up, down, g_gains)]
    row = lanes_of([sum(grad)] + [total_of(ref[...]) for ref in masters])
    sums[...] = jnp.broadcast_to(row[None], sums.shape)


def whole(ref_or_array):
    return pl.BlockSpec(memory_space=pltpu.VMEM)


def grads(masters, swapped, merge, down, devices, heads, docs):
    inputs = [*masters, swapped, merge, down]
    return pl.pallas_call(
        functools.partial(grads_kernel, heads, docs),
        in_specs=[whole(member) for member in inputs],
        out_specs=[whole(None)] * 5,
        out_shape=[
            jax.ShapeDtypeStruct(masters[0].shape, F32),
            jax.ShapeDtypeStruct(masters[2].shape, F32),
            jax.ShapeDtypeStruct(masters[3].shape, F32),
            jax.ShapeDtypeStruct(masters[5].shape, F32),
            jax.ShapeDtypeStruct((devices, 1, LANES), F32),
        ],
        compiler_params=params(),
        cost_estimate=cheap(),
        name="grads",
    )(*inputs)


def moments_kernel(*refs):
    totals, refs = refs[0], refs[1:]
    masters, old_moments, old_squares, gradients = (refs[6 * j : 6 * j + 6] for j in range(4))
    moments, squares, directions = (refs[6 * j - 19 : 6 * j - 13] for j in range(3))
    sums = refs[-1]
    total = jnp.sum(totals[...], axis=0)
    factor = CLIP / jnp.maximum(jnp.sqrt(total[:, 0:1]), CLIP)
    fix_one = 1.0 - BETA_ONE**STEP
    fix_two = 1.0 - BETA_TWO**STEP
    norms = []
    for place in range(6):
        clipped = factor * gradients[place][...]
        moment = BETA_ONE * old_moments[place][...] + (1.0 - BETA_ONE) * clipped
        square = BETA_TWO * old_squares[place][...] + (1.0 - BETA_TWO) * clipped * clipped
        direction = moment / fix_one / (jnp.sqrt(square / fix_two) + ADAM_EPS)
        if place < 5:
            direction = direction + DECAY * masters[place][...]
        moments[place][...] = moment
        squares[place][...] = square
        directions[place][...] = direction
        norms.append(total_of(direction))
    sums[...] = jnp.broadcast_to(lanes_of(norms)[None], sums.shape)


def step_moments(totals, masters, moments, squares, gradients, waits):
    inputs = [totals, *masters, *moments, *squares, *gradients]
    shapes = [jax.ShapeDtypeStruct(member.shape, F32) for member in masters]
    out = pl.pallas_call(
        moments_kernel,
        in_specs=[whole(member) for member in inputs] + waits_for(len(waits)),
        out_specs=[whole(None)] * 19,
        out_shape=shapes * 3 + [jax.ShapeDtypeStruct(totals.shape, F32)],
        compiler_params=params(),
        cost_estimate=cheap(),
        name="moments",
    )(*inputs, *waits)
    return out[:6], out[6:12], out[12:18], out[18]


def weights_kernel(*refs):
    totals, updates, refs = refs[0], refs[1], refs[2:]
    masters, directions, fresh = refs[:6], refs[6:12], refs[-8:-2]
    norms, clip = refs[-2:]
    old = jnp.sqrt(jnp.sum(totals[...], axis=0))
    new = jnp.sqrt(jnp.sum(updates[...], axis=0))
    for place in range(6):
        trust = old[:, place + 1 : place + 2] / new[:, place : place + 1]
        fresh[place][...] = masters[place][...] - RATE * trust * directions[place][...]
    norms[0:1, :] = pltpu.roll(old, LANES - 1, 1)
    norms[1:2, :] = new
    clip[...] = old


def step_weights(totals, updates, masters, directions, waits):
    inputs = [totals, updates, *masters, *directions]
    shapes = [jax.ShapeDtypeStruct(member.shape, F32) for member in masters]
    out = pl.pallas_call(
        weights_kernel,
        in_specs=[whole(member) for member in inputs] + waits_for(len(waits)),
        out_specs=[whole(None)] * 8,
        out_shape=shapes
        + [jax.ShapeDtypeStruct((2, LANES), F32), jax.ShapeDtypeStruct((1, LANES), F32)],
        compiler_params=params(),
        cost_estimate=cheap(),
        name="weights",
    )(*inputs, *waits)
    return out[:6], out[6][:, :6], out[7][0, 0]


def norm_rows(values):
    row_scale = lax.rsqrt(jnp.mean(values * values, axis=-1, keepdims=True) + NORM_EPS)
    return (values * row_scale, row_scale)


def norm_back(grad_normed, unit_rows, row_scale, gain_row):
    weighted = grad_normed * gain_row
    inner = jnp.mean(weighted * unit_rows, axis=-1, keepdims=True)
    return row_scale * (weighted - unit_rows * inner)


def rotation(length):
    half = HEAD_DIM // 2
    frequency = jnp.exp(-jnp.log(10000.0) * jnp.arange(half, dtype=F32) / half)
    grid = jnp.arange(length, dtype=F32)[:, None] * frequency[None, :]
    cos, sin = jnp.cos(grid), jnp.sin(grid)
    return jnp.concatenate([cos, cos], 1), jnp.concatenate([-sin, sin], 1)


def shards(
    tokens, cotangent, cache_keys, cache_values, neighbours, partner, has_memory,
    w_heads, moment_heads, square_heads, w_merge, moment_merge, square_merge,
    w_gate, moment_gate, square_gate, w_up, moment_up, square_up,
    w_down, moment_down, square_down, gains, moment_gains, square_gains,
):
    _, rows, width = tokens.shape
    seq_count = lax.axis_size("seq")
    docs_count = lax.axis_size("docs")
    devices = seq_count * docs_count
    seq_index = lax.axis_index("seq")
    doc_index = lax.axis_index("docs")
    here = jnp.stack([seq_index, doc_index]).astype(jnp.int32)
    length = rows * seq_count
    heads = HEADS // seq_count
    cols = heads * HEAD_DIM
    weight_rows = w_heads.shape[0]
    down_rows = w_down.shape[0]
    group = -(-down_rows // 16) * 16
    hidden = group * docs_count
    per_device = cache_keys.shape[1]
    masters = (w_heads, w_merge, w_gate, w_up, w_down, gains)
    moments = (moment_heads, moment_merge, moment_gate, moment_up, moment_down, moment_gains)
    squares = (square_heads, square_merge, square_gate, square_up, square_down, square_gains)

    low_heads = w_heads.astype(BF).reshape(weight_rows, 3, seq_count, heads, HEAD_DIM)
    low_heads = low_heads.transpose(2, 0, 3, 1, 4).reshape(seq_count, weight_rows, 3 * cols)
    gain_cols = jnp.pad(gains.astype(BF).T, ((0, 0), (0, LANES - 2)))
    first_pieces = swap(
        lambda j: jnp.concatenate(
            [lax.dynamic_index_in_dim(low_heads, j, 0, False), gain_cols], axis=1
        )
    )
    first_block = stack(first_pieces, "seq")
    merge_cols = width // seq_count
    low_merge = w_merge.astype(BF).reshape(weight_rows, seq_count, merge_cols).transpose(1, 0, 2)
    low_merge = low_merge.reshape(seq_count * weight_rows, merge_cols)
    first = pieces_of(jnp.concatenate([first_block, low_merge], axis=1), "docs")


    def columns(member):
        split = member.astype(BF).reshape(weight_rows, docs_count, seq_count, down_rows)
        split = jnp.pad(split.transpose(2, 0, 1, 3), ((0, 0), (0, 0), (0, 0), (0, group - down_rows)))
        return split.reshape(seq_count, weight_rows, hidden)

    low_raw = after(jnp.concatenate([columns(w_gate), columns(w_up)], axis=2), first_block)
    raw_pieces = swap(lambda j: lax.dynamic_index_in_dim(low_raw, j, 0, False))
    low_raw = stack(raw_pieces, "seq")
    packed = pack_inner(low_raw, w_down, group, min(512, width))
    packed = pieces_of(packed, "docs")

    near = jnp.concatenate([neighbours[0] // 64, neighbours[0] % 64], axis=1).astype(BF)
    x_near = pieces_of(after(jnp.concatenate([tokens[0], near], axis=1), low_raw), "seq")
    flag = jnp.take(has_memory, doc_index[None])
    grad_low = pieces_of(after(cotangent[0], x_near[2 if seq_count > 2 else -1]), "seq")
    low_merge = stack([piece[:, 3 * cols + LANES :] for piece in first], "docs")
    low_merge = low_merge.reshape(docs_count, seq_count, weight_rows, merge_cols)
    low_merge = low_merge.transpose(0, 2, 1, 3).reshape(docs_count, weight_rows, width)
    low_merge = pieces_of(low_merge, "seq")
    merge_full = jnp.stack([pick(low_merge, "seq", j) for j in range(seq_count)], axis=1)
    merge_full = merge_full.reshape(width, width)

    small = [send(packed[k][:16], "docs", 1) for k in range(2, len(packed), 4)]
    waits = (*first_pieces[1:], *raw_pieces[1:])
    gated, memory = [], []
    for member in pack_memory(partner, cache_keys, cache_values, heads, seq_count):
        gated.append(gate(member.reshape(devices, 2, per_device, 2 * HEAD_DIM), *waits))
        member = lax.all_to_all(
            gated[-1], ("docs", "seq"), split_axis=0, concat_axis=0, tiled=True
        )
        memory.append(member.reshape(devices * 2 * per_device, 2 * HEAD_DIM))
        waits = (
            memory[0], *first[1:], *packed[1:3], *small, *x_near[1:], *grad_low[1:], *low_merge[1:]
        )
    grad_low = lay_out(here, grad_low)
    cosine, sine = rotation(length)
    (
        x_low, normed_one, query_local, query_memory, key_local, value_local, words, heads_here, gain_rows,
    ) = project(here, x_near, first, cosine, sine, heads, per_device * devices, per_device,
      gated[-1:])
    local, high, total = attend_local(query_local, key_local, value_local, heads)


    attended, blended, lse = [], [], []
    waits = (grad_low, merge_full)
    for h in range(heads):
        result = attend_memory(
            flag, query_memory, words, memory[h], local, high, total, h, waits
        )
        attended.append(result[0])
        blended.append(pieces_of(result[1], "seq"))
        lse.append(result[2])

    blended, normed_two, active, grad_raw, back, middle, _, down_here = feed_forward(
        here, [piece for pieces in zip(*blended) for piece in pieces], packed,
        x_low, merge_full, gain_rows, grad_low, heads, hidden,
    )
    bits = docs_count.bit_length() - 1
    g_raw = dot_tn(normed_two, grad_raw).astype(BF)
    g_raw = g_raw.reshape(docs_count, width // docs_count, 2 * hidden)
    grad_normed_two = halve(back.reshape(seq_count, rows, width), "seq", 0)
    started = token(grad_normed_two)
    g_down = (dot_tn(active, grad_low) + started).astype(BF).reshape(docs_count, group, width)
    down_out = (dot(active, down_here) + started).astype(BF).reshape(seq_count, rows, width)
    grad_normed_two = reduce_over(grad_normed_two, "seq", 1)
    unit_two, scale_two = norm_rows(middle)
    grad_middle = cotangent[0].astype(F32) + norm_back(
        grad_normed_two, unit_two, scale_two, gain_rows[1:2]
    )
    grad_branch = grad_middle.astype(BF)
    grad_mine = dot_nt(grad_branch, merge_full).astype(BF)
    grad_attended = stack(swap(lambda j: lax.dynamic_slice_in_dim(grad_mine, j * cols, cols, 1)), "seq")

    arrived = token(grad_attended)
    x_bits = bits // 2
    first_z = [(stage, 1 << x_bits) for stage in range(x_bits, bits)]
    first_z += [(stage, 1) for stage in range(x_bits)]
    g_down = halve(g_down, "docs", first_z[0][0], arrived, first_z[0][1])
    g_raw = halve(g_raw, "docs", 0, arrived)
    waits = (g_raw, g_down)
    branches = pieces_of(gate(grad_branch, grad_attended), "seq")

    projected, g_heads = [], []
    for h in range(heads):
        projected.append(
            attend_back(
                flag, query_local, query_memory, key_local, value_local, words,
                memory[h], attended[h], grad_attended, lse[h], cosine, sine, h, waits,
            )
        )
        g_head = dot_tn(normed_one, projected[h]).astype(BF)
        g_head = g_head.reshape(docs_count, width // docs_count, 3 * HEAD_DIM)
        if h == 0:
            halfway = token(projected[0])
            g_merge = (dot_tn(blended, stack(branches, "seq")) + halfway).astype(BF)
            g_merge = g_merge.reshape(docs_count, seq_count, weight_rows, width)
            g_merge = lax.dynamic_index_in_dim(g_merge, seq_index, 1, False)
            down_out = halve(down_out, "seq", 0, halfway)
            g_raw = halve(g_raw, "docs", 1, halfway)
            waits = (g_head, g_merge)
        g_heads.append(g_head)
    last = token(projected[-1])
    g_heads = [halve(member, "docs", 0, last) for member in g_heads[::-1]]
    arrived = token(g_heads[0])
    g_heads = halve(jnp.concatenate(g_heads, axis=2), "docs", 1)
    g_merge = halve(g_merge, "docs", 0, arrived)
    g_merge = reduce_over(halve(g_merge, "docs", 1, token(g_heads)), "docs", 2)
    for k in range(2, bits):
        g_raw = halve(g_raw, "docs", k, last if k == 2 else 0.0)
    for k in range(1, bits):
        late = last if k == 1 else 0.0
        g_down = halve(g_down, "docs", first_z[k][0], late, first_z[k][1])
    g_heads = reduce_over(g_heads, "docs", 2)
    g_down = g_down[0][:down_rows]
    g_raw = jnp.concatenate([g_raw[0], g_heads], axis=1)
    g_raw = g_raw.astype(BF).reshape(seq_count, weight_rows, 2 * hidden + 3 * cols)
    g_raw = stack(swap(lambda j: lax.dynamic_index_in_dim(g_raw, j, 0, False)), "seq")
    g_heads, g_gate, g_up, g_gains, totals = grads(
        masters, g_raw, g_merge, g_down, devices, heads, docs_count
    )
    gradients = (g_heads, g_merge, g_gate, g_up, g_down, g_gains)
    totals = to_everyone(totals)
    grad_projected = jnp.concatenate(projected, axis=1)
    grad_normed_one = (dot_nt(grad_projected, heads_here) + arrived).astype(BF)
    grad_normed_one = halve(grad_normed_one.reshape(seq_count, rows, width), "seq", 0)
    new_moments, new_squares, directions, updates = step_moments(
        totals, masters, moments, squares, gradients, ()
    )
    moved = token(updates)
    grad_normed_one = reduce_over(grad_normed_one, "seq", 1, moved)
    unit_one, scale_one = norm_rows(tokens[0].astype(F32))
    input_grad = grad_middle + norm_back(grad_normed_one, unit_one, scale_one, gain_rows[0:1])
    input_grad = input_grad[None]
    down_out = reduce_over(down_out, "seq", 1, moved)
    activations = (middle + down_out).astype(BF)[None]

    new_weights, layer_norms, clip_norm = step_weights(
        totals, to_everyone(updates), masters, directions, (input_grad, activations)
    )
    results = [activations, input_grad]
    for place in range(6):
        results += [new_moments[place], new_squares[place], new_weights[place]]
    return (*results, clip_norm, layer_norms)


def solution(mesh):
    by_token = P("docs", "seq", None)
    by_slot = P(None, ("docs", "seq"), None)
    by_row = P(("docs", "seq"), None)
    by_gain = P(None, ("docs", "seq"))
    return jax.shard_map(
        shards,
        mesh=mesh,
        in_specs=(by_token, by_token, by_slot, by_slot, by_token, P(), P())
        + (by_row,) * 15
        + (by_gain,) * 3,
        out_specs=(by_token, by_token) + (by_row,) * 15 + (by_gain,) * 3 + (P(), P()),
        check_vma=False,
    )
```

```python
import functools
import math

import jax
import jax.numpy as jnp
from jax import lax
from jax.experimental import pallas as pl
from jax.experimental.pallas import tpu as pltpu
from jax.sharding import PartitionSpec as P

HEADS = 8
HEAD_DIM = 128
STEP = 10
NORM_EPS = 1e-06
BETA_ONE = 0.9
BETA_TWO = 0.999
ADAM_EPS = 1e-06
DECAY = 0.01
RATE = 0.5
CLIP = 1.0
LANES = 128
LOG2E = math.log2(math.e)
SCALE = HEAD_DIM ** (-0.5)
BF = jnp.bfloat16
F32 = jnp.float32


def send(x, axis, bits):
    return lax.ppermute(x, axis, [(i, i ^ bits) for i in range(lax.axis_size(axis))])


def token(*done):
    total = jnp.zeros((), F32)
    for member in done:
        corner = lax.slice(member, (0,) * member.ndim, (1,) * member.ndim)
        total = total + corner.reshape(()).astype(F32) * 0
    return total


def after(x, *done):
    return x + token(*done).astype(x.dtype)


def pieces_of(block, axis):
    bit = lax.axis_size(axis) // 2
    pieces = {0: block}
    while bit:
        pieces.update({k | bit: send(piece, axis, bit) for k, piece in list(pieces.items())})
        bit //= 2
    return [pieces[k] for k in range(len(pieces))]


def pick(pieces, axis, device):
    away = lax.axis_index(axis) ^ device
    picked = pieces[0]
    for k in range(1, len(pieces)):
        picked = jnp.where(away == k, pieces[k], picked)
    return picked


def stack(pieces, axis, dim=0):
    return jnp.concatenate([pick(pieces, axis, j) for j in range(len(pieces))], axis=dim)


def swap(cut):
    me = lax.axis_index("seq")
    return [cut(me)] + [send(cut(me ^ k), "seq", k) for k in range(1, lax.axis_size("seq"))]


def halve(blocks, axis, stage, late=0.0, low=1):
    mine = (lax.axis_index(axis) >> stage) & 1
    pairs = blocks.reshape((-1, 2, low) + blocks.shape[1:])
    away = lax.dynamic_index_in_dim(pairs, 1 - mine, 1, False).astype(BF)
    kept = lax.dynamic_index_in_dim(pairs, mine, 1, False).astype(F32)
    total = (kept + late) + send(away, axis, 1 << stage).astype(F32)
    return total.reshape((-1,) + blocks.shape[1:])


def reduce_over(blocks, axis, stage=0, late=0.0):
    while blocks.shape[0] > 1:
        blocks = halve(blocks, axis, stage, late if blocks.shape[0] == 2 else 0.0)
        stage += 1
    return blocks[0]


def to_everyone(vectors):
    return lax.all_to_all(vectors, ("docs", "seq"), split_axis=0, concat_axis=0, tiled=True)


def dot(a, b):
    return lax.dot_general(a, b, (((1,), (0,)), ((), ())), preferred_element_type=F32)


def dot_nt(a, b):
    return lax.dot_general(a, b, (((1,), (1,)), ((), ())), preferred_element_type=F32)


def dot_tn(a, b):
    return lax.dot_general(a, b, (((0,), (0,)), ((), ())), preferred_element_type=F32)


def params(mebibytes=56):
    return pltpu.CompilerParams(vmem_limit_bytes=mebibytes * 1024 * 1024)


def rows_of(rows, cols):
    return pl.BlockSpec((rows, cols), lambda i: (i, 0))


def all_of(rows, cols):
    return pl.BlockSpec((rows, cols), lambda i: (0, 0))


def cheap():
    return pl.CostEstimate(flops=1, bytes_accessed=1, transcendentals=0)


def waits_for(count):
    return [pl.BlockSpec(memory_space=pl.ANY)] * count


def gate_kernel(*refs):
    pass


def gate(x, *waits):
    return pl.pallas_call(
        gate_kernel,
        in_specs=waits_for(1 + len(waits)),
        out_specs=pl.BlockSpec(memory_space=pl.ANY),
        out_shape=jax.ShapeDtypeStruct(x.shape, x.dtype),
        input_output_aliases={0: 0},
        cost_estimate=cheap(),
        name="gate",
    )(x, *waits)


def pack_memory_kernel(heads, partner, key, value, mate_key, mate_value, *outs):
    for device in range(outs[0].shape[1]):
        for h in range(heads):
            at = slice((device * heads + h) * HEAD_DIM, (device * heads + h + 1) * HEAD_DIM)
            outs[h][0, device, 0, :, :HEAD_DIM] = key[0, :, at]
            outs[h][0, device, 0, :, HEAD_DIM:] = value[0, :, at]
            outs[h][0, device, 1, :, :HEAD_DIM] = mate_key[0, :, at]
            outs[h][0, device, 1, :, HEAD_DIM:] = mate_value[0, :, at]


def pack_memory(partner, cache_keys, cache_values, heads, seq_count):
    docs, rows, width = cache_keys.shape
    own = pl.BlockSpec((1, rows, width), lambda i, p: (i, 0, 0))
    mate = pl.BlockSpec((1, rows, width), lambda i, p: (p[i], 0, 0))
    shape = (docs, seq_count, 2, rows, 2 * HEAD_DIM)
    return pl.pallas_call(
        functools.partial(pack_memory_kernel, heads),
        grid_spec=pltpu.PrefetchScalarGridSpec(
            num_scalar_prefetch=1,
            grid=(docs,),
            in_specs=[own, own, mate, mate],
            out_specs=[pl.BlockSpec((1,) + shape[1:], lambda i, p: (i, 0, 0, 0, 0))] * heads,
        ),
        out_shape=[jax.ShapeDtypeStruct(shape, BF)] * heads,
        compiler_params=params(),
        cost_estimate=cheap(),
        name="pack_memory",
    )(partner, cache_keys, cache_values, cache_keys, cache_values)


def pack_inner_kernel(raw, down, out):
    part = out.shape[1]
    at = 0
    for c in range(raw.shape[1] // part):
        out[at : at + raw.shape[0], :] = raw[:, c * part : (c + 1) * part]
        at += raw.shape[0]
    group = (out.shape[0] - at) // (down.shape[1] // part)
    rest = jnp.zeros((group - down.shape[0], part), F32)
    for c in range(down.shape[1] // part):
        rows = jnp.concatenate([down[:, c * part : (c + 1) * part], rest], axis=0)
        out[at : at + group, :] = rows.astype(BF)
        at += group


def pack_inner(raw, down, group, part):
    rows = raw.shape[0] * (raw.shape[1] // part) + group * (down.shape[1] // part)
    return pl.pallas_call(
        pack_inner_kernel,
        in_specs=[whole(raw), whole(down)],
        out_specs=whole(None),
        out_shape=jax.ShapeDtypeStruct((rows, part), BF),
        cost_estimate=cheap(),
        name="pack_inner",
    )(raw, down)


def rows_at(ref, place, rows):
    return ref.at[pl.ds(pl.multiple_of(place * rows, rows), rows)]


def whole_spec(member):
    return pl.BlockSpec(member.shape, lambda i, here, n=member.ndim: (0,) * n)


def tile_spec(rows, cols):
    return pl.BlockSpec((rows, cols), lambda i, here: (i, 0))


def fixed_spec(rows, cols):
    return pl.BlockSpec((rows, cols), lambda i, here: (0, 0))


def lay_kernel(here, *refs):
    pieces, out = refs[:-1], refs[-1]
    for k, piece in enumerate(pieces):

        @pl.when(here[0] ^ k == pl.program_id(0))
        def _(piece=piece):
            out[...] = piece[...]


def lay_out(here, pieces):
    rows, cols = pieces[0].shape
    return pl.pallas_call(
        lay_kernel,
        grid_spec=pltpu.PrefetchScalarGridSpec(
            num_scalar_prefetch=1,
            grid=(len(pieces),),
            in_specs=[whole_spec(piece) for piece in pieces],
            out_specs=tile_spec(rows, cols),
        ),
        out_shape=jax.ShapeDtypeStruct((len(pieces) * rows, cols), pieces[0].dtype),
        compiler_params=params(),
        cost_estimate=cheap(),
        name="lay_out",
    )(here, *pieces)


def find_words(near, memory, per_device):
    wide = near.astype(F32).T.astype(jnp.int32)
    count = wide.shape[0] // 2
    index = wide[:count] * 64 + wide[count:]
    slot = index & (memory - 1)
    source = slot >> (per_device.bit_length() - 1)
    place = source * (2 * per_device) + (slot & (per_device - 1))
    place = place + (index >> (memory.bit_length() - 1)) * per_device
    bit = jnp.left_shift(jnp.int32(1), place >> 7)
    lane = place & (LANES - 1)
    shape = (LANES, near.shape[0])
    rows = lax.broadcasted_iota(jnp.int32, shape, 0)
    found = jnp.zeros(shape, jnp.int32)
    for n in range(count):
        found = found | jnp.where(rows == lane[n : n + 1], bit[n : n + 1], 0)
    return found.T


def project_kernel(heads, seq, docs, memory, per_device, here, *refs):
    tokens, weights = refs[:seq], refs[seq : seq + docs]
    cosine, sine = refs[seq + docs : seq + docs + 2]
    x, normed, ql, qm, kl, vl, words, weight, gains, held = refs[-10:]
    width = x.shape[1]
    cols = 3 * heads * HEAD_DIM
    step = pl.program_id(0)

    @pl.when(step == 0)
    def _():
        for k in range(docs):
            rows = weights[k].shape[0]
            rows_at(weight, here[1] ^ k, rows)[...] = weights[k][:, :cols]
            rows_at(held, here[1] ^ k, rows)[...] = weights[k][:, cols : cols + LANES].astype(F32)
        for part in range(width // LANES):
            lanes = slice(part * LANES, (part + 1) * LANES)
            gains[:, lanes] = held[lanes, :].T[: gains.shape[0]]

    for k in range(seq):

        @pl.when(here[0] ^ k == step)
        def _(k=k):
            x[...] = tokens[k][:, :width]
            words[...] = find_words(tokens[k][:, width:], memory, per_device)

    values = x[...].astype(F32)
    scale = lax.rsqrt(jnp.mean(values * values, axis=-1, keepdims=True) + NORM_EPS)
    low = (values * scale * gains[0:1, :]).astype(BF)
    normed[...] = low
    out = dot(low, weight[...])
    cos, sin = cosine[...], sine[...]
    for h in range(heads):
        part = slice(h * HEAD_DIM, (h + 1) * HEAD_DIM)
        q, k, v = (
            out[:, (3 * h + j) * HEAD_DIM : (3 * h + j + 1) * HEAD_DIM] for j in range(3)
        )
        qm[:, part] = q.astype(BF)
        ql[:, part] = (q * cos + pltpu.roll(q, HEAD_DIM // 2, 1) * sin).astype(BF)
        kl[:, part] = (k * cos + pltpu.roll(k, HEAD_DIM // 2, 1) * sin).astype(BF)
        vl[:, part] = v.astype(BF)


def project(here, tokens, weights, cosine, sine, heads, memory, per_device, waits):
    rows = tokens[0].shape[0]
    width = tokens[0].shape[1] - LANES
    length = rows * len(tokens)
    cols = heads * HEAD_DIM
    low = jax.ShapeDtypeStruct((length, cols), BF)
    full = jax.ShapeDtypeStruct((length, width), BF)
    return pl.pallas_call(
        functools.partial(project_kernel, heads, len(tokens), len(weights), memory, per_device),
        grid_spec=pltpu.PrefetchScalarGridSpec(
            num_scalar_prefetch=1,
            grid=(len(tokens),),
            in_specs=[whole_spec(member) for member in (*tokens, *weights)]
            + [tile_spec(rows, HEAD_DIM)] * 2
            + waits_for(len(waits)),
            out_specs=[tile_spec(rows, width)] * 2
            + [tile_spec(rows, cols)] * 4
            + [tile_spec(rows, LANES), fixed_spec(width, 3 * cols), fixed_spec(8, width)],
            scratch_shapes=[pltpu.VMEM((width, LANES), F32)],
        ),
        out_shape=[
            full, full, low, low, low, low,
            jax.ShapeDtypeStruct((length, LANES), jnp.int32),
            jax.ShapeDtypeStruct((width, 3 * cols), BF),
            jax.ShapeDtypeStruct((8, width), F32),
        ],
        compiler_params=params(),
        cost_estimate=cheap(),
        name="project",
    )(here, *tokens, *weights, cosine, sine, *waits)


def feed_forward_kernel(heads, seq, docs, here, *refs):
    blended, packed, refs = refs[: seq * heads], refs[seq * heads :][:docs], refs[seq * heads + docs :]
    x, merge, gains, cotangent = refs[:4]
    blend, normed, active, grad_raw, back, middle_mine, raw, down = refs[4:]
    step = pl.program_id(0)
    hidden = down.shape[0]
    part = packed[0].shape[1]
    rows, group = raw.shape[0] // docs, hidden // docs

    @pl.when(step == 0)
    def _():
        for k in range(docs):
            at = 0
            for c in range(raw.shape[1] // part):
                cols = slice(c * part, (c + 1) * part)
                rows_at(raw, here[1] ^ k, rows)[:, cols] = packed[k][at : at + rows, :]
                at += rows
            for c in range(down.shape[1] // part):
                cols = slice(c * part, (c + 1) * part)
                rows_at(down, here[1] ^ k, group)[:, cols] = packed[k][at : at + group, :]
                at += group

    for k in range(seq):
        for h in range(heads):
            at = pl.multiple_of(((here[0] ^ k) * heads + h) * HEAD_DIM, HEAD_DIM)
            blend[:, pl.ds(at, HEAD_DIM)] = blended[k * heads + h][...]
    middle = x[...].astype(F32) + dot(blend[...], merge[...])

    @pl.when(step == here[0])
    def _():
        middle_mine[...] = middle

    scale = lax.rsqrt(jnp.mean(middle * middle, axis=-1, keepdims=True) + NORM_EPS)
    low = (middle * scale * gains[1:2, :]).astype(BF)
    normed[...] = low
    grad_active = dot_nt(cotangent[...], down[...])
    gate_up = dot(low, raw[...])
    gate, up = gate_up[:, :hidden], gate_up[:, hidden:]
    sigmoid = jax.nn.sigmoid(gate)
    silu = gate * sigmoid
    active[...] = (silu * up).astype(BF)
    grad_gate = grad_active * up * sigmoid * (1.0 + gate * (1.0 - sigmoid))
    grad_raw[:, :hidden] = grad_gate.astype(BF)
    grad_raw[:, hidden:] = (grad_active * silu).astype(BF)
    back[...] = dot_nt(grad_raw[...], raw[...]).astype(BF)


def feed_forward(here, blended, packed, x, merge, gains, cotangent, heads, hidden):
    length, width = x.shape
    seq, docs = len(blended) // heads, len(packed)
    rows = length // seq
    double = 2 * hidden
    return pl.pallas_call(
        functools.partial(feed_forward_kernel, heads, seq, docs),
        grid_spec=pltpu.PrefetchScalarGridSpec(
            num_scalar_prefetch=1,
            grid=(seq,),
            in_specs=[tile_spec(rows, HEAD_DIM)] * len(blended)
            + [whole_spec(member) for member in packed]
            + [tile_spec(rows, width), whole_spec(merge), whole_spec(gains)]
            + [tile_spec(rows, width)],
            out_specs=[
                tile_spec(rows, width),
                tile_spec(rows, width),
                tile_spec(rows, hidden),
                tile_spec(rows, double),
                tile_spec(rows, width),
                fixed_spec(rows, width),
                fixed_spec(width, double),
                fixed_spec(hidden, width),
            ],
        ),
        out_shape=[
            jax.ShapeDtypeStruct((length, width), BF),
            jax.ShapeDtypeStruct((length, width), BF),
            jax.ShapeDtypeStruct((length, hidden), BF),
            jax.ShapeDtypeStruct((length, double), BF),
            jax.ShapeDtypeStruct((length, width), BF),
            jax.ShapeDtypeStruct((rows, width), F32),
            jax.ShapeDtypeStruct((width, double), BF),
            jax.ShapeDtypeStruct((hidden, width), BF),
        ],
        compiler_params=params(),
        cost_estimate=cheap(),
        name="feed_forward",
    )(here, *blended, *packed, x, merge, gains, cotangent)


def lower_triangle(span):
    row = lax.broadcasted_iota(jnp.int32, (span, span), 0)
    return lax.broadcasted_iota(jnp.int32, (span, span), 1) <= row


def allowed(words, chunk, chunk_keys):
    tiles = chunk_keys // LANES
    parts = []
    for tile in range(tiles):
        bit = chunk * tiles + tile
        mask = (1 << bit) if bit < 31 else -(1 << 31)
        parts.append((words & jnp.int32(mask)) != 0)
    return parts


def select_tiles(parts, values, other):
    cut = [
        jnp.where(part, values[:, t * LANES : (t + 1) * LANES], other)
        for t, part in enumerate(parts)
    ]
    return jnp.concatenate(cut, axis=1)


def attend_local_kernel(heads, tiles, ql, kl, vl, out, high, total):
    span = ql.shape[0]
    factor = SCALE * LOG2E

    for tile in range(tiles):

        @pl.when(pl.program_id(0) == tile)
        def _(tile=tile):
            seen = lower_triangle(span)
            for h in range(heads):
                part = slice(h * HEAD_DIM, (h + 1) * HEAD_DIM)
                keys = (tile + 1) * span
                scores = dot_nt(ql[:, part], kl[:keys, part]) * factor
                last = jnp.where(seen, scores[:, tile * span :], -jnp.inf)
                scores = jnp.concatenate([scores[:, : tile * span], last], 1) if tile else last
                top = jnp.max(scores, axis=1, keepdims=True)
                expo = jnp.exp2(scores - top)
                high[:, part] = jnp.broadcast_to(top, (span, HEAD_DIM))
                weight = jnp.sum(expo, axis=1, keepdims=True)
                total[:, part] = jnp.broadcast_to(weight, (span, HEAD_DIM))
                out[:, part] = dot(expo.astype(BF), vl[:keys, part])


def attend_local(ql, kl, vl, heads):
    length, width = ql.shape
    span = min(512, length)
    wide = jax.ShapeDtypeStruct((length, width), F32)
    return pl.pallas_call(
        functools.partial(attend_local_kernel, heads, length // span),
        grid=(length // span,),
        in_specs=[rows_of(span, width), all_of(length, width), all_of(length, width)],
        out_specs=[rows_of(span, width)] * 3,
        out_shape=[wide] * 3,
        compiler_params=params(),
        cost_estimate=cheap(),
        name="attend_local",
    )(ql, kl, vl)


def attend_memory_kernel(chunk_keys, flag, qm, words, kv, local, high, total, *refs):
    out, low, lse = refs[-3:]
    factor = SCALE * LOG2E

    def finish(top, weight, sums):
        values = sums / weight
        out[...] = values
        low[...] = values.astype(BF)
        lse[...] = jnp.broadcast_to(top + jnp.log2(weight), lse.shape)

    @pl.when(flag[0] == 0)
    def _():
        finish(high[:, :1], total[:, :1], local[...])

    @pl.when(flag[0] > 0)
    def _():
        bits = words[...]
        query = qm[...]
        top, weight, sums = high[:, :1], total[:, :1], local[...]
        for chunk in range(kv.shape[0] // chunk_keys):
            here = slice(chunk * chunk_keys, (chunk + 1) * chunk_keys)
            scores = dot_nt(query, kv[here, :HEAD_DIM]) * factor
            scores = select_tiles(allowed(bits, chunk, chunk_keys), scores, -jnp.inf)
            new_top = jnp.maximum(top, jnp.max(scores, axis=1, keepdims=True))
            shrink = jnp.exp2(top - new_top)
            expo = jnp.exp2(scores - new_top)
            weight = weight * shrink + jnp.sum(expo, axis=1, keepdims=True)
            sums = sums * shrink + dot(expo.astype(BF), kv[here, HEAD_DIM:])
            top = new_top
        finish(top, weight, sums)


def head_rows(span, head):
    return pl.BlockSpec((span, HEAD_DIM), lambda i: (i, head))


def head_all(length, head):
    return pl.BlockSpec((length, HEAD_DIM), lambda i: (0, head))


def attend_memory(flag, qm, words, kv, local, high, total, head, waits):
    length = qm.shape[0]
    span = min(512, length)
    keys = kv.shape[0]
    return pl.pallas_call(
        functools.partial(attend_memory_kernel, min(4096, keys)),
        grid=(length // span,),
        in_specs=[
            pl.BlockSpec(memory_space=pltpu.SMEM),
            head_rows(span, head),
            rows_of(span, LANES),
            all_of(keys, 2 * HEAD_DIM),
            head_rows(span, head),
            head_rows(span, head),
            head_rows(span, head),
            *waits_for(len(waits)),
        ],
        out_specs=[rows_of(span, HEAD_DIM)] * 3,
        out_shape=[
            jax.ShapeDtypeStruct((length, HEAD_DIM), F32),
            jax.ShapeDtypeStruct((length, HEAD_DIM), BF),
            jax.ShapeDtypeStruct((length, HEAD_DIM), F32),
        ],
        compiler_params=params(),
        cost_estimate=cheap(),
        name="attend_memory",
    )(flag, qm, words, kv, local, high, total, *waits)


def attend_back_kernel(
    chunk_keys, tiles, flag, ql, qm, kl, vl, words, kv, att, go, lse, cosq, sinq, cosk, sink, *refs
):
    out, sum_k, sum_v, sum_q = refs[-4:]
    span = ql.shape[0]
    factor = SCALE * LOG2E
    step = pl.program_id(0)
    grad = go[...]
    delta = jnp.sum(grad.astype(F32) * att[...], axis=1, keepdims=True)
    level = lse[:, :1]

    @pl.when(step == 0)
    def _():
        sum_k[...] = jnp.zeros_like(sum_k)
        sum_v[...] = jnp.zeros_like(sum_v)

    for tile in range(tiles):

        @pl.when(step == tile)
        def _(tile=tile):
            keys = (tile + 1) * span
            query = ql[...]
            scores = dot_nt(query, kl[:keys]) * factor
            prob = jnp.exp2(scores - level)
            last = jnp.where(lower_triangle(span), prob[:, tile * span :], 0.0)
            prob = jnp.concatenate([prob[:, : tile * span], last], 1) if tile else last
            grad_prob = dot_nt(grad, vl[:keys])
            grad_scores = (prob * (grad_prob - delta)).astype(BF)
            sum_v[:keys] += dot_tn(prob.astype(BF), grad)
            sum_k[:keys] += dot_tn(grad_scores, query)
            back = dot(grad_scores, kl[:keys])
            sum_q[...] = back * cosq[...] - pltpu.roll(back, HEAD_DIM // 2, 1) * sinq[...]

    @pl.when(flag[0] > 0)
    def _():
        bits = words[...]
        query = qm[...]
        sums = sum_q[...]
        for chunk in range(kv.shape[0] // chunk_keys):
            here = slice(chunk * chunk_keys, (chunk + 1) * chunk_keys)
            key = kv[here, :HEAD_DIM]
            scores = dot_nt(query, key) * factor
            prob = jnp.exp2(scores - level)
            prob = select_tiles(allowed(bits, chunk, chunk_keys), prob, 0.0)
            grad_prob = dot_nt(grad, kv[here, HEAD_DIM:])
            grad_scores = (prob * (grad_prob - delta)).astype(BF)
            sums = sums + dot(grad_scores, key)
        sum_q[...] = sums

    here = pl.ds(pl.multiple_of(step * span, span), span)
    out[here, :HEAD_DIM] = (sum_q[...] * SCALE).astype(BF)

    @pl.when(step == tiles - 1)
    def _():
        back = sum_k[...] * SCALE
        back = back * cosk[...] - pltpu.roll(back, HEAD_DIM // 2, 1) * sink[...]
        out[:, HEAD_DIM : 2 * HEAD_DIM] = back.astype(BF)
        out[:, 2 * HEAD_DIM :] = sum_v[...].astype(BF)


def attend_back(flag, ql, qm, kl, vl, words, kv, att, go, lse, cosine, sine, head, waits):
    length, width = ql.shape
    span = min(512, length)
    keys = kv.shape[0]
    return pl.pallas_call(
        functools.partial(attend_back_kernel, min(512, keys), length // span),
        grid=(length // span,),
        in_specs=[
            pl.BlockSpec(memory_space=pltpu.SMEM),
            head_rows(span, head),
            head_rows(span, head),
            head_all(length, head),
            head_all(length, head),
            rows_of(span, LANES),
            all_of(keys, 2 * HEAD_DIM),
            rows_of(span, HEAD_DIM),
            head_rows(span, head),
            rows_of(span, HEAD_DIM),
            rows_of(span, HEAD_DIM),
            rows_of(span, HEAD_DIM),
            all_of(length, HEAD_DIM),
            all_of(length, HEAD_DIM),
            *waits_for(len(waits)),
        ],
        out_specs=all_of(length, 3 * HEAD_DIM),
        out_shape=jax.ShapeDtypeStruct((length, 3 * HEAD_DIM), BF),
        scratch_shapes=[
            pltpu.VMEM((length, HEAD_DIM), F32),
            pltpu.VMEM((length, HEAD_DIM), F32),
            pltpu.VMEM((span, HEAD_DIM), F32),
        ],
        compiler_params=params(),
        cost_estimate=pl.CostEstimate(
            flops=16 * 10**9, bytes_accessed=8 * length * width, transcendentals=length * keys
        ),
        name="attend_back",
    )(flag, ql, qm, kl, vl, words, kv, att, go, lse, cosine, sine, cosine, sine, *waits)


def total_of(member):
    return jnp.sum(jnp.sum(member * member, axis=1, keepdims=True), axis=0, keepdims=True)


def lanes_of(values):
    lane = lax.broadcasted_iota(jnp.int32, (1, LANES), 1)
    row = jnp.zeros((1, LANES), F32)
    for place, value in enumerate(values):
        row = jnp.where(lane == place, value, row)
    return row


def row_of(column):
    shape = (column.shape[0], column.shape[0])
    same = lax.broadcasted_iota(jnp.int32, shape, 0) == lax.broadcasted_iota(jnp.int32, shape, 1)
    return jnp.sum(jnp.where(same, column, 0.0), axis=0, keepdims=True)


def grads_kernel(heads, docs, *refs):
    masters = refs[:6]
    swapped, merge, down, g_heads, gate, up, g_gains, sums = refs[6:]
    rows = g_heads.shape[0]
    width = g_heads.shape[1] // 3
    seq = swapped.shape[0] // rows
    cols = 3 * HEAD_DIM * heads
    group, part = (swapped.shape[1] - cols) // (2 * docs), gate.shape[1] // (docs * seq)
    for device in range(seq):
        lines = slice(device * rows, (device + 1) * rows)
        for h in range(heads):
            for j in range(3):
                at = swapped.shape[1] - cols + (3 * (heads - 1 - h) + j) * HEAD_DIM
                to = j * width + (device * heads + h) * HEAD_DIM
                g_heads[:, to : to + HEAD_DIM] = swapped[lines, at : at + HEAD_DIM].astype(F32)
        for d in range(docs):
            to = (d * seq + device) * part
            for j, target in enumerate((gate, up)):
                at = (j * docs + d) * group
                target[:, to : to + part] = swapped[lines, at : at + part].astype(F32)
    low = masters[0][...].astype(BF).astype(F32)
    gain_one = jnp.sum(g_heads[...] * low, axis=1, keepdims=True)
    gain_two = jnp.sum(
        gate[...] * masters[2][...].astype(BF).astype(F32)
        + up[...] * masters[3][...].astype(BF).astype(F32),
        axis=1,
        keepdims=True,
    )
    gain_low = masters[5][...].astype(BF).astype(F32)
    g_gains[0:1, :] = row_of(gain_one) / gain_low[0:1]
    g_gains[1:2, :] = row_of(gain_two) / gain_low[1:2]
    grad = [total_of(ref[...]) for ref in (g_heads, merge, gate, up, down, g_gains)]
    row = lanes_of([sum(grad)] + [total_of(ref[...]) for ref in masters])
    sums[...] = jnp.broadcast_to(row[None], sums.shape)


def whole(ref_or_array):
    return pl.BlockSpec(memory_space=pltpu.VMEM)


def grads(masters, swapped, merge, down, devices, heads, docs):
    inputs = [*masters, swapped, merge, down]
    return pl.pallas_call(
        functools.partial(grads_kernel, heads, docs),
        in_specs=[whole(member) for member in inputs],
        out_specs=[whole(None)] * 5,
        out_shape=[
            jax.ShapeDtypeStruct(masters[0].shape, F32),
            jax.ShapeDtypeStruct(masters[2].shape, F32),
            jax.ShapeDtypeStruct(masters[3].shape, F32),
            jax.ShapeDtypeStruct(masters[5].shape, F32),
            jax.ShapeDtypeStruct((devices, 1, LANES), F32),
        ],
        compiler_params=params(),
        cost_estimate=cheap(),
        name="grads",
    )(*inputs)


def moments_kernel(*refs):
    totals, refs = refs[0], refs[1:]
    masters, old_moments, old_squares, gradients = (refs[6 * j : 6 * j + 6] for j in range(4))
    moments, squares, directions = (refs[6 * j - 19 : 6 * j - 13] for j in range(3))
    sums = refs[-1]
    total = jnp.sum(totals[...], axis=0)
    factor = CLIP / jnp.maximum(jnp.sqrt(total[:, 0:1]), CLIP)
    fix_one = 1.0 - BETA_ONE**STEP
    fix_two = 1.0 - BETA_TWO**STEP
    norms = []
    for place in range(6):
        clipped = factor * gradients[place][...]
        moment = BETA_ONE * old_moments[place][...] + (1.0 - BETA_ONE) * clipped
        square = BETA_TWO * old_squares[place][...] + (1.0 - BETA_TWO) * clipped * clipped
        direction = moment / fix_one / (jnp.sqrt(square / fix_two) + ADAM_EPS)
        if place < 5:
            direction = direction + DECAY * masters[place][...]
        moments[place][...] = moment
        squares[place][...] = square
        directions[place][...] = direction
        norms.append(total_of(direction))
    sums[...] = jnp.broadcast_to(lanes_of(norms)[None], sums.shape)


def step_moments(totals, masters, moments, squares, gradients, waits):
    inputs = [totals, *masters, *moments, *squares, *gradients]
    shapes = [jax.ShapeDtypeStruct(member.shape, F32) for member in masters]
    out = pl.pallas_call(
        moments_kernel,
        in_specs=[whole(member) for member in inputs] + waits_for(len(waits)),
        out_specs=[whole(None)] * 19,
        out_shape=shapes * 3 + [jax.ShapeDtypeStruct(totals.shape, F32)],
        compiler_params=params(),
        cost_estimate=cheap(),
        name="moments",
    )(*inputs, *waits)
    return out[:6], out[6:12], out[12:18], out[18]


def weights_kernel(*refs):
    totals, updates, refs = refs[0], refs[1], refs[2:]
    masters, directions, fresh = refs[:6], refs[6:12], refs[-8:-2]
    norms, clip = refs[-2:]
    old = jnp.sqrt(jnp.sum(totals[...], axis=0))
    new = jnp.sqrt(jnp.sum(updates[...], axis=0))
    for place in range(6):
        trust = old[:, place + 1 : place + 2] / new[:, place : place + 1]
        fresh[place][...] = masters[place][...] - RATE * trust * directions[place][...]
    norms[0:1, :] = pltpu.roll(old, LANES - 1, 1)
    norms[1:2, :] = new
    clip[...] = old


def step_weights(totals, updates, masters, directions, waits):
    inputs = [totals, updates, *masters, *directions]
    shapes = [jax.ShapeDtypeStruct(member.shape, F32) for member in masters]
    out = pl.pallas_call(
        weights_kernel,
        in_specs=[whole(member) for member in inputs] + waits_for(len(waits)),
        out_specs=[whole(None)] * 8,
        out_shape=shapes
        + [jax.ShapeDtypeStruct((2, LANES), F32), jax.ShapeDtypeStruct((1, LANES), F32)],
        compiler_params=params(),
        cost_estimate=cheap(),
        name="weights",
    )(*inputs, *waits)
    return out[:6], out[6][:, :6], out[7][0, 0]


def norm_rows(values):
    row_scale = lax.rsqrt(jnp.mean(values * values, axis=-1, keepdims=True) + NORM_EPS)
    return (values * row_scale, row_scale)


def norm_back(grad_normed, unit_rows, row_scale, gain_row):
    weighted = grad_normed * gain_row
    inner = jnp.mean(weighted * unit_rows, axis=-1, keepdims=True)
    return row_scale * (weighted - unit_rows * inner)


def rotation(length):
    half = HEAD_DIM // 2
    frequency = jnp.exp(-jnp.log(10000.0) * jnp.arange(half, dtype=F32) / half)
    grid = jnp.arange(length, dtype=F32)[:, None] * frequency[None, :]
    cos, sin = jnp.cos(grid), jnp.sin(grid)
    return jnp.concatenate([cos, cos], 1), jnp.concatenate([-sin, sin], 1)


def shards(
    tokens, cotangent, cache_keys, cache_values, neighbours, partner, has_memory,
    w_heads, moment_heads, square_heads, w_merge, moment_merge, square_merge,
    w_gate, moment_gate, square_gate, w_up, moment_up, square_up,
    w_down, moment_down, square_down, gains, moment_gains, square_gains,
):
    _, rows, width = tokens.shape
    seq_count = lax.axis_size("seq")
    docs_count = lax.axis_size("docs")
    devices = seq_count * docs_count
    seq_index = lax.axis_index("seq")
    doc_index = lax.axis_index("docs")
    here = jnp.stack([seq_index, doc_index]).astype(jnp.int32)
    length = rows * seq_count
    heads = HEADS // seq_count
    cols = heads * HEAD_DIM
    weight_rows = w_heads.shape[0]
    down_rows = w_down.shape[0]
    group = -(-down_rows // 16) * 16
    hidden = group * docs_count
    per_device = cache_keys.shape[1]
    masters = (w_heads, w_merge, w_gate, w_up, w_down, gains)
    moments = (moment_heads, moment_merge, moment_gate, moment_up, moment_down, moment_gains)
    squares = (square_heads, square_merge, square_gate, square_up, square_down, square_gains)

    low_heads = w_heads.astype(BF).reshape(weight_rows, 3, seq_count, heads, HEAD_DIM)
    low_heads = low_heads.transpose(2, 0, 3, 1, 4).reshape(seq_count, weight_rows, 3 * cols)
    gain_cols = jnp.pad(gains.astype(BF).T, ((0, 0), (0, LANES - 2)))
    first_pieces = swap(
        lambda j: jnp.concatenate(
            [lax.dynamic_index_in_dim(low_heads, j, 0, False), gain_cols], axis=1
        )
    )
    first_block = stack(first_pieces, "seq")
    merge_cols = width // seq_count
    low_merge = w_merge.astype(BF).reshape(weight_rows, seq_count, merge_cols).transpose(1, 0, 2)
    low_merge = low_merge.reshape(seq_count * weight_rows, merge_cols)
    first = pieces_of(jnp.concatenate([first_block, low_merge], axis=1), "docs")


    def columns(member):
        split = member.astype(BF).reshape(weight_rows, docs_count, seq_count, down_rows)
        split = jnp.pad(split.transpose(2, 0, 1, 3), ((0, 0), (0, 0), (0, 0), (0, group - down_rows)))
        return split.reshape(seq_count, weight_rows, hidden)

    low_raw = jnp.concatenate([columns(w_gate), columns(w_up)], axis=2)
    raw_pieces = swap(lambda j: lax.dynamic_index_in_dim(low_raw, j, 0, False))
    low_raw = stack(raw_pieces, "seq")
    packed = pack_inner(low_raw, w_down, group, min(512, width))
    packed = pieces_of(packed, "docs")

    near = jnp.concatenate([neighbours[0] // 64, neighbours[0] % 64], axis=1).astype(BF)
    x_near = pieces_of(gate(jnp.concatenate([tokens[0], near], axis=1), *raw_pieces[1:]), "seq")
    flag = jnp.take(has_memory, doc_index[None])
    grad_low = pieces_of(gate(cotangent[0], x_near[2 if seq_count > 2 else -1]), "seq")
    low_merge = stack([piece[:, 3 * cols + LANES :] for piece in first], "docs")
    low_merge = low_merge.reshape(docs_count, seq_count, weight_rows, merge_cols)
    low_merge = low_merge.transpose(0, 2, 1, 3).reshape(docs_count, weight_rows, width)
    low_merge = pieces_of(low_merge, "seq")
    merge_full = jnp.stack([pick(low_merge, "seq", j) for j in range(seq_count)], axis=1)
    merge_full = merge_full.reshape(width, width)

    small = [send(packed[k][:16], "docs", 1) for k in range(2, len(packed), 4)]
    waits = (*first_pieces[1:], *raw_pieces[1:])
    gated, memory = [], []
    for member in pack_memory(partner, cache_keys, cache_values, heads, seq_count):
        gated.append(gate(member.reshape(devices, 2, per_device, 2 * HEAD_DIM), *waits))
        member = lax.all_to_all(
            gated[-1], ("docs", "seq"), split_axis=0, concat_axis=0, tiled=True
        )
        memory.append(member.reshape(devices * 2 * per_device, 2 * HEAD_DIM))
        waits = (
            memory[0], *first[1:], *packed[1:3], *small, *x_near[1:], *grad_low[1:], *low_merge[1:]
        )
    grad_low = lay_out(here, grad_low)
    cosine, sine = rotation(length)
    (
        x_low, normed_one, query_local, query_memory, key_local, value_local, words, heads_here, gain_rows,
    ) = project(here, x_near, first, cosine, sine, heads, per_device * devices, per_device,
      gated[-1:])
    local, high, total = attend_local(query_local, key_local, value_local, heads)


    attended, blended, lse = [], [], []
    waits = (grad_low, merge_full)
    for h in range(heads):
        result = attend_memory(
            flag, query_memory, words, memory[h], local, high, total, h, waits
        )
        attended.append(result[0])
        blended.append(pieces_of(result[1], "seq"))
        lse.append(result[2])

    blended, normed_two, active, grad_raw, back, middle, _, down_here = feed_forward(
        here, [piece for pieces in zip(*blended) for piece in pieces], packed,
        x_low, merge_full, gain_rows, grad_low, heads, hidden,
    )
    bits = docs_count.bit_length() - 1
    g_raw = dot_tn(normed_two, grad_raw).astype(BF)
    g_raw = g_raw.reshape(docs_count, width // docs_count, 2 * hidden)
    grad_normed_two = halve(back.reshape(seq_count, rows, width), "seq", 0)
    started = token(grad_normed_two)
    g_down = (dot_tn(active, grad_low) + started).astype(BF).reshape(docs_count, group, width)
    down_out = (dot(active, down_here) + started).astype(BF).reshape(seq_count, rows, width)
    grad_normed_two = reduce_over(grad_normed_two, "seq", 1)
    unit_two, scale_two = norm_rows(middle)
    grad_middle = cotangent[0].astype(F32) + norm_back(
        grad_normed_two, unit_two, scale_two, gain_rows[1:2]
    )
    grad_branch = grad_middle.astype(BF)
    grad_mine = dot_nt(grad_branch, merge_full).astype(BF)
    grad_attended = stack(swap(lambda j: lax.dynamic_slice_in_dim(grad_mine, j * cols, cols, 1)), "seq")

    arrived = token(grad_attended)
    x_bits = bits // 2
    first_z = [(stage, 1 << x_bits) for stage in range(x_bits, bits)]
    first_z += [(stage, 1) for stage in range(x_bits)]
    g_down = halve(g_down, "docs", first_z[0][0], arrived, first_z[0][1])
    g_raw = halve(g_raw, "docs", 0, arrived)
    waits = (g_raw, g_down)
    branches = pieces_of(gate(grad_branch, grad_attended), "seq")

    projected, g_heads = [], []
    for h in range(heads):
        projected.append(
            attend_back(
                flag, query_local, query_memory, key_local, value_local, words,
                memory[h], attended[h], grad_attended, lse[h], cosine, sine, h, waits,
            )
        )
        g_head = dot_tn(normed_one, projected[h]).astype(BF)
        g_head = g_head.reshape(docs_count, width // docs_count, 3 * HEAD_DIM)
        if h == 0:
            halfway = token(projected[0])
            g_merge = (dot_tn(blended, stack(branches, "seq")) + halfway).astype(BF)
            g_merge = g_merge.reshape(docs_count, seq_count, weight_rows, width)
            g_merge = lax.dynamic_index_in_dim(g_merge, seq_index, 1, False)
            down_out = halve(down_out, "seq", 0, halfway)
            g_raw = halve(g_raw, "docs", 1, halfway)
            waits = (g_head, g_merge)
        g_heads.append(g_head)
    last = token(projected[-1])
    g_heads = [halve(member, "docs", 0, last) for member in g_heads[::-1]]
    arrived = token(g_heads[0])
    g_heads = halve(jnp.concatenate(g_heads, axis=2), "docs", 1)
    g_merge = halve(g_merge, "docs", 0, arrived)
    g_merge = reduce_over(halve(g_merge, "docs", 1, token(g_heads)), "docs", 2)
    for k in range(2, bits):
        g_raw = halve(g_raw, "docs", k, last if k == 2 else 0.0)
    for k in range(1, bits):
        late = last if k == 1 else token(g_heads)
        g_down = halve(g_down, "docs", first_z[k][0], late, first_z[k][1])
    g_heads = reduce_over(g_heads, "docs", 2)
    g_down = g_down[0][:down_rows]
    g_raw = jnp.concatenate([g_raw[0], g_heads], axis=1)
    g_raw = g_raw.astype(BF).reshape(seq_count, weight_rows, 2 * hidden + 3 * cols)
    g_raw = stack(swap(lambda j: lax.dynamic_index_in_dim(g_raw, j, 0, False)), "seq")
    g_heads, g_gate, g_up, g_gains, totals = grads(
        masters, g_raw, g_merge, g_down, devices, heads, docs_count
    )
    gradients = (g_heads, g_merge, g_gate, g_up, g_down, g_gains)
    totals = to_everyone(totals)
    grad_projected = jnp.concatenate(projected, axis=1)
    grad_normed_one = (dot_nt(grad_projected, heads_here) + arrived).astype(BF)
    grad_normed_one = halve(grad_normed_one.reshape(seq_count, rows, width), "seq", 0)
    new_moments, new_squares, directions, updates = step_moments(
        totals, masters, moments, squares, gradients, ()
    )
    moved = token(updates)
    grad_normed_one = reduce_over(grad_normed_one, "seq", 1, moved)
    unit_one, scale_one = norm_rows(tokens[0].astype(F32))
    input_grad = grad_middle + norm_back(grad_normed_one, unit_one, scale_one, gain_rows[0:1])
    input_grad = input_grad[None]
    down_out = reduce_over(down_out, "seq", 1, moved)
    activations = (middle + down_out).astype(BF)[None]

    new_weights, layer_norms, clip_norm = step_weights(
        totals, to_everyone(updates), masters, directions, (input_grad, activations)
    )
    results = [activations, input_grad]
    for place in range(6):
        results += [new_moments[place], new_squares[place], new_weights[place]]
    return (*results, clip_norm, layer_norms)


def solution(mesh):
    by_token = P("docs", "seq", None)
    by_slot = P(None, ("docs", "seq"), None)
    by_row = P(("docs", "seq"), None)
    by_gain = P(None, ("docs", "seq"))
    return jax.shard_map(
        shards,
        mesh=mesh,
        in_specs=(by_token, by_token, by_slot, by_slot, by_token, P(), P())
        + (by_row,) * 15
        + (by_gain,) * 3,
        out_specs=(by_token, by_token) + (by_row,) * 15 + (by_gain,) * 3 + (P(), P()),
        check_vma=False,
    )
```
